32 devices in a mesh: sector: 8 (over z, x), band: 4 (over y, core).
Axes of the slice: x: 2, y: 2, z: 4, core: 2. Of those that a mesh axis runs over, the one named last changes fastest.
Arguments:
- orbitals: bfloat16 [8, 32, 16, 4096], P('sector', None, None, 'band'), may hold values from -216 to 216
- potential: float32 [8, 32, 16], P('sector'), may hold values from 0.1 to 3
- near_points: int32 [128, 48], P('sector'), may hold values from 0 to 511
- near_values: bfloat16 [128, 48], P('sector'), may hold values from -0.875 to 0.875
- far_points: int32 [128, 16], P('sector'), may hold values from 0 to 511
- far_values: bfloat16 [128, 16], P('sector'), may hold values from -1.5 to 1.5
- atom_energy: float32 [128], P('sector'), may hold values from -1 to 2
Outputs:
- ham_panel: float32 [2048, 4096], P('sector', 'band')
- gram_panel: float32 [2048, 4096], P('sector', 'band')
The draws below stay inside these ranges and needn't reach their ends.
Inputs may be any that keep to these rules, and one draw needn't show every extreme that they name: `near_points`: indices of points of the owning slab. `far_points`: row block s names points of slab s's first plane, for the atoms owned by slab s - 1 (mod 8).
All inputs are finite; a program needn't handle non-finite values.
Results may differ from the reference program's by a relative error of at most 0.00039.
Values may be sent and summed in bfloat16 or wider, within the bound.
A program may use at most 64 MiB of HBM per device.

```python
import math
import jax
import jax.numpy as jnp
from jax import lax

A_DEV = 1
NR = 32
NZ = 16
TWIST = 3
ORB = 4096
PANEL = 2048
ATOM_DEV = 16
SUP_NEAR = 48
SUP_FAR = 16
NA = 8
PLANE = 512
PTS_DEV = 512
NG = 4096
ORB_DEV = 1024
PANEL_DEV = 512
ATOMS = 128
N_SECTOR = 8
N_BAND = 4


def draw_orbitals(key, part):
    key_noise = jax.random.fold_in(key, 11)
    key_fields = jax.random.fold_in(key, 12)
    key_mix = jax.random.fold_in(key, 13)
    key_rows = jax.random.fold_in(key, 14)
    key_cols = jax.random.fold_in(key, 15)
    noise = jnp.clip(jax.random.normal(key_noise, (NA, NR, NZ, ORB), jnp.float32), -4.0, 4.0)
    row_scale = jnp.exp(jax.random.uniform(key_rows, (NA, NR, NZ, 1), jnp.float32, jnp.log(0.3), jnp.log(3.0)))
    fields = jnp.clip(jax.random.normal(key_fields, (4, NA, NR, NZ, 1), jnp.float32), -4.0, 4.0)
    mixing = jnp.clip(0.5 * jax.random.normal(key_mix, (4, ORB), jnp.float32), -2.0, 2.0)
    col_scale = jnp.exp(jax.random.uniform(key_cols, (ORB,), jnp.float32, jnp.log(0.5), jnp.log(2.0)))
    total = noise
    total = total + fields[0] * mixing[0]
    total = total + fields[1] * mixing[1]
    total = total + fields[2] * mixing[2]
    total = total + fields[3] * mixing[3]
    return (row_scale * total * col_scale).astype(jnp.bfloat16)


def set_ends(drawn, own_key, low, high):
    index_at = [jax.random.randint(jax.random.fold_in(own_key, axis), (), 0, length) for axis, length in enumerate(drawn.shape)]
    widest = drawn.shape.index(max(drawn.shape))
    beside = index_at[:widest] + [(index_at[widest] + 1) % drawn.shape[widest]] + index_at[widest + 1:]
    return drawn.at[tuple(index_at)].set(low).at[tuple(beside)].set(high)


def block_scale(stream_key, extent, split, least, largest):
    loudness, own = 1.0, jax.random.fold_in(stream_key, 6)
    for dim, parts in split:
        heights = jnp.exp(jax.random.uniform(jax.random.fold_in(own, dim), (parts,), jnp.float32, least / len(split), largest / len(split)))
        loudness = loudness * jnp.repeat(heights, extent[dim] // parts).reshape([-1 if axis == dim else 1 for axis in range(len(extent))])
    return loudness


def gaussian(rng, dims, scale, reach, cuts=(), kind=jnp.bfloat16):
    result = scale * jax.random.normal(rng, dims, jnp.float32)
    if cuts:
        result = result * block_scale(rng, dims, cuts, -0.22, 0.18)
    return jnp.clip(result, -reach, reach).astype(kind)


def setup_inputs(seed: int = 0) -> dict:
    arg_keys = jax.random.split(jax.random.key(seed), 8)
    return {
        "orbitals": draw_orbitals(jax.random.fold_in(arg_keys[7], 71), 0),
        "potential": jnp.clip(jnp.exp(math.log(3.0) - 3.4011974 * jax.random.uniform(arg_keys[1], (NA, NR, NZ), jnp.float32) ** block_scale(arg_keys[1], (NA, NR, NZ), ((0, 8),), -0.2, 0.2)), 0.1, 3.0),
        "near_points": set_ends(jax.random.randint(arg_keys[2], (ATOMS, SUP_NEAR), 0, PTS_DEV), jax.random.fold_in(arg_keys[2], 1), 0, PTS_DEV - 1).astype(jnp.int32),
        "near_values": gaussian(arg_keys[3], (ATOMS, SUP_NEAR), SUP_NEAR ** -0.5, 0.875, ((0, 8),)),
        "far_points": set_ends(jax.random.randint(arg_keys[4], (ATOMS, SUP_FAR), 0, PLANE), jax.random.fold_in(arg_keys[4], 1), 0, PLANE - 1).astype(jnp.int32),
        "far_values": gaussian(arg_keys[5], (ATOMS, SUP_FAR), SUP_FAR ** -0.5, 1.5, ((0, 8),)),
        "atom_energy": jnp.clip(-1.0 + 3.0 * jax.random.uniform(arg_keys[6], (ATOMS,), jnp.float32) ** block_scale(arg_keys[6], (ATOMS,), ((0, 8),), -0.2, 0.2), -1.0, 2.0),
    }


CENTER = 6.0
HALF_SPAN = 3.0


def build_dense(points, values, width):
    column_ids = jnp.arange(width, dtype=jnp.int32)
    matches = (points[:, :, None] == column_ids[None, None, :]).astype(jnp.float32)
    return jnp.sum(matches * values.astype(jnp.float32)[:, :, None], axis=1).astype(jnp.bfloat16)


def apply_operator(field_in, potential, near_dense, far_dense, atom_energy):
    wavefunc = field_in.astype(jnp.float32)
    upper_plane = jnp.roll(wavefunc[0], -TWIST, axis=1)
    lower_plane = jnp.roll(wavefunc[-1], TWIST, axis=1)
    angular = jnp.concatenate([wavefunc[1:], upper_plane[None]], 0) + jnp.concatenate([lower_plane[None], wavefunc[:-1]], 0) - 2.0 * wavefunc
    zero_rim = jnp.zeros_like(wavefunc[:, :1])
    outer_rad = jnp.concatenate([wavefunc[:, 1:], zero_rim], 1)
    inner_rad = jnp.concatenate([zero_rim, wavefunc[:, :-1]], 1)
    radius = (NR + jnp.arange(NR, dtype=jnp.float32))[None, :, None, None]
    radial = outer_rad + inner_rad - 2.0 * wavefunc + (outer_rad - inner_rad) / (2.0 * radius)
    axial_sum = jnp.roll(wavefunc, 1, axis=2) + jnp.roll(wavefunc, -1, axis=2) - 2.0 * wavefunc
    weight = (NR / radius) ** 2
    kinetic = -0.5 * (radial + axial_sum + weight * angular)
    slabs = field_in.reshape(N_SECTOR, PTS_DEV, -1).astype(jnp.float32)
    near_f = near_dense.astype(jnp.float32)
    far_f = far_dense.astype(jnp.float32)
    near_coef = jnp.einsum('sap,spo->sao', near_f, slabs)
    first_planes = field_in.reshape(N_SECTOR, A_DEV, PLANE, -1)[:, 0].astype(jnp.float32)
    far_coef = jnp.einsum('sap,spo->sao', far_f, first_planes)
    coeffs = near_coef + jnp.roll(far_coef, -1, axis=0)
    scaled = atom_energy.reshape(N_SECTOR, ATOM_DEV)[:, :, None] * coeffs
    spread = jnp.einsum('sap,sao->spo', near_f, scaled, precision=lax.Precision.HIGHEST)
    back_add = jnp.einsum('sap,sao->spo', far_f, jnp.roll(scaled, 1, axis=0), precision=lax.Precision.HIGHEST)
    spread = spread.reshape(N_SECTOR, A_DEV, PLANE, -1)
    spread = spread.at[:, 0].add(back_add)
    nonlocal_term = spread.reshape(NA, NR, NZ, -1)
    return kinetic + potential[..., None] * wavefunc + nonlocal_term


def reference(orbitals, potential, near_points, near_values, far_points, far_values, atom_energy):
    near_dense = lax.map(lambda pair: build_dense(pair[0], pair[1], PTS_DEV),
                         (near_points.reshape(N_SECTOR, ATOM_DEV, SUP_NEAR), near_values.reshape(N_SECTOR, ATOM_DEV, SUP_NEAR)))
    far_dense = lax.map(lambda pair: build_dense(pair[0], pair[1], PLANE),
                        (far_points.reshape(N_SECTOR, ATOM_DEV, SUP_FAR), far_values.reshape(N_SECTOR, ATOM_DEV, SUP_FAR)))
    blocks = orbitals.reshape(NA, NR, NZ, N_BAND, ORB_DEV).transpose(3, 0, 1, 2, 4)

    def operate(field_in):
        return apply_operator(field_in, potential, near_dense, far_dense, atom_energy)

    def filter_block(block):
        block32 = block.astype(jnp.float32)
        first = ((operate(block) - CENTER * block32) / HALF_SPAN).astype(jnp.bfloat16)
        filtered = (2.0 * (operate(first) - CENTER * first.astype(jnp.float32)) / HALF_SPAN - block32).astype(jnp.bfloat16)
        image = operate(filtered).astype(jnp.bfloat16)
        return filtered.reshape(NG, ORB_DEV), image.reshape(NG, ORB_DEV)

    filtered_all, images_all = lax.map(filter_block, blocks)
    panel = filtered_all[:, :, :PANEL_DEV].transpose(1, 0, 2).reshape(NG, PANEL).astype(jnp.float32)

    def project(pair):
        filtered_b, image_b = pair
        ham_b = jnp.dot(panel.T, image_b.astype(jnp.float32), precision=lax.Precision.HIGHEST)
        gram_b = jnp.dot(panel.T, filtered_b.astype(jnp.float32), precision=lax.Precision.HIGHEST)
        return ham_b, gram_b

    hams, grams = lax.map(project, (filtered_all, images_all))
    ham_panel = hams.transpose(1, 0, 2).reshape(PANEL, ORB) / NG
    gram_panel = grams.transpose(1, 0, 2).reshape(PANEL, ORB) / NG
    return ham_panel, gram_panel
```

```python
import functools

import jax
import jax.numpy as jnp
import numpy as np
from jax import lax
from jax.experimental import pallas as pl
from jax.experimental.pallas import tpu as pltpu
from jax.sharding import PartitionSpec as P

MESH = pl.DeviceIdType.MESH
F32 = jnp.float32
BF16 = jnp.bfloat16

TWIST = 3
PANEL = 2048
CENTER = 6.0
HALF_SPAN = 3.0
LANES = 128
BLOCK = 64


def widen(tile, width):
    return jnp.concatenate([tile] * (width // LANES), axis=1) if width > LANES else tile


def kernel(n, nb, nr, nz, chunk, batches, orb, npts, nval, fpts, fval, energy, pot, base, shifts, ham, gram,
           O, A, F, I, BB, W, B, EB, CO, SP, PB, PT, PH, PG, RH, RG,
           xs, xr, zs, zr, ps, pr, os, orr):
    plane, cols = orb.shape
    rows = ham.shape[0]
    atoms, near_sup = npts.shape
    far_sup = fpts.shape[1]
    half = plane // 2
    mine = cols // 2
    chunks = mine // chunk
    levels = n // 2
    panel_dev = PANEL // nb
    panel_blocks = panel_dev // LANES
    pieces = max(panel_blocks // 2, 1)
    both = panel_blocks >= 2
    order = list(range(pieces)) + ([panel_blocks + j for j in range(pieces)] if both else [])
    window = BLOCK + 2 * nz
    per_block = BLOCK // nz
    s = lax.axis_index("sector")
    b = lax.axis_index("band")
    x = lax.rem(s, 2)
    level = s // 2
    partner = s + 1 - 2 * x
    core = lax.rem(b, 2)
    sibling = b + 1 - 2 * core
    owner = level

    def source_lane(j, side):
        return pl.multiple_of((order[j] + side * pieces) * LANES, LANES)

    def remote(src, dst, send, recv, **device):
        return pltpu.make_async_remote_copy(
            src_ref=src, dst_ref=dst, send_sem=send, recv_sem=recv, device_id=device, device_id_type=MESH)

    def target(way):
        return s + 2 if way == 0 else s - 2

    def has_target(way):
        return level + 1 < levels if way == 0 else level >= 1

    def has_source(way, d):
        return level - d >= 0 if way == 0 else level + d < levels

    def source_level(way, d):
        return level - d if way == 0 else level + d

    barrier = pltpu.get_barrier_semaphore()
    pl.semaphore_signal(barrier, inc=1, device_id={"sector": partner}, device_id_type=MESH)
    for way in range(2):
        @pl.when(has_target(way))
        def _():
            pl.semaphore_signal(barrier, inc=1, device_id={"sector": target(way)}, device_id_type=MESH)
    for d in range(1, nb):
        pl.semaphore_signal(barrier, inc=1, device_id={"band": lax.rem(b + d, nb)}, device_id_type=MESH)

    eye = lax.broadcasted_iota(jnp.int32, (atoms, atoms), 0) == lax.broadcasted_iota(jnp.int32, (atoms, atoms), 1)
    column = jnp.sum(jnp.where(eye, jnp.broadcast_to(energy[...], (atoms, atoms)), 0.0), axis=1, keepdims=True)
    BB[s, 0:atoms, :] = jnp.concatenate(
        [npts[...].astype(F32), nval[...].astype(F32), fpts[...].astype(F32), fval[...].astype(F32)], axis=1)
    BB[s, atoms:2 * atoms, :] = jnp.concatenate(
        [pot[...], jnp.broadcast_to(column, (atoms, LANES - nr))], axis=1)
    ends = jnp.where(level == 0, 1, 0) + jnp.where(level == levels - 1, 1, 0)
    pl.semaphore_wait(barrier, nb + 2 - ends)

    per = chunk // LANES

    def place(c, p, count):
        if c == chunks:
            return BB.at[p] if count == 1 else BB.at[pl.ds(p, count)]
        rows_at, lanes_at = pl.ds(nz, plane), pl.ds(c * chunk, chunk)
        return O.at[p + 1, rows_at, lanes_at] if count == 1 else O.at[pl.ds(p + 1, count), rows_at, lanes_at]

    def own_source(c, side):
        return BB.at[s] if c == chunks else orb.at[:, pl.ds(source_lane(c * per, side), chunk)]

    def cross(c):
        return remote(own_source(c, 1 - x), place(c, s, 1), xs.at[c], xr.at[c], sector=partner)

    def cross_wait(c):
        remote(place(c, partner, 1), place(c, partner, 1), xs.at[c], xr.at[c], sector=partner).wait_recv()

    def direct(c, j, way):
        dst = place(c, s if j == 0 else partner, 1)
        return remote(own_source(c, x) if j == 0 else dst, dst,
                      zs.at[way, c, 0, j], zr.at[way, c, 0, j], sector=target(way))

    def relay(c, way, d):
        ref = place(c, 2 * source_level(way, d), 2)
        return remote(ref, ref, zs.at[way, c, d, 0], zr.at[way, c, d, 0], sector=target(way))

    def arrived(c, way, d):
        lv = source_level(way, d)
        if d == 1:
            for j in range(2):
                ref = place(c, 2 * lv + (x if j == 0 else 1 - x), 1)
                remote(ref, ref, zs.at[way, c, 0, j], zr.at[way, c, 0, j], sector=partner).wait_recv()
        else:
            ref = place(c, 2 * lv, 2)
            remote(ref, ref, zs.at[way, c, d - 1, 0], zr.at[way, c, d - 1, 0], sector=partner).wait_recv()

    def send_plane(c, j, act):
        for way in range(2):
            @pl.when(has_target(way))
            def _():
                act(direct(c, j, way))

    pumped = set()

    def pump(c, d):
        if c > chunks or d >= levels - 1 or (c, d) in pumped:
            return
        pumped.add((c, d))
        for way in range(2):
            @pl.when(has_source(way, d) & has_target(way))
            def _():
                arrived(c, way, d)
                relay(c, way, d).start()

    def gather(c):
        for d in range(1, levels):
            pump(c, d)
        for d in range(1, levels):
            for way in range(2):
                here = has_source(way, d)
                if d < levels - 1:
                    here = here & jnp.logical_not(has_target(way))

                @pl.when(here)
                def _():
                    arrived(c, way, d)

    def start(copy):
        copy.start()

    crossed = set()

    def send_own(c):
        if c >= chunks:
            return
        send_plane(c, 0, start)
        cross_wait(c)
        crossed.add(c)
        send_plane(c, 1, start)

    cross(chunks).start()
    for c in range(chunks):
        cross(c).start()
    send_plane(chunks, 0, start)
    send_plane(0, 0, start)
    for j in range(mine // LANES):
        O[s + 1, nz:nz + plane, j * LANES:(j + 1) * LANES] = orb[:, pl.ds(source_lane(j, x), LANES)]
    cross_wait(chunks)
    send_plane(chunks, 1, start)
    cross_wait(0)
    send_plane(0, 1, start)
    send_own(1)

    for ref, width in ((O, mine), (F, mine), (A, chunk)):
        @pl.loop(0, n)
        def _(p):
            ref[p + 1, 0:nz, :] = jnp.zeros((nz, width), BF16)
            ref[p + 1, nz + plane:nz + plane + nz, :] = jnp.zeros((nz, width), BF16)

    def setup():
        lane = lax.broadcasted_iota(jnp.int32, (BLOCK, 2 * LANES), 1)
        row = lax.broadcasted_iota(jnp.int32, (BLOCK, 2 * LANES), 0)
        diagonal = (lane == row + nz) | (lane == row + nz + window)
        ids = lax.broadcasted_iota(jnp.int32, (atoms, plane), 1).astype(F32)

        @pl.loop(0, n)
        def _(p):
            packed = BB[p, 0:atoms, :]

            def dense(at, count):
                total = jnp.zeros((atoms, plane), F32)
                for j in range(count):
                    point = packed[:, at + j:at + j + 1]
                    value = packed[:, at + count + j:at + count + j + 1]
                    total = total + jnp.where(ids == point, value, 0.0)
                return total.astype(BF16).astype(F32)

            near = dense(0, near_sup)
            far = dense(2 * near_sup, far_sup)
            both_parts = jnp.concatenate([near, far], axis=0)
            W[p] = both_parts.astype(BF16)
            turned = jnp.concatenate([both_parts] * (LANES // (2 * atoms)), axis=0).T
            local = BB[p, atoms:2 * atoms, :]
            EB[p] = jnp.broadcast_to(local[:, nr:nr + 1] * (1.0 / HALF_SPAN), (atoms, LANES))
            for q in range(plane // BLOCK):
                at = slice(q * BLOCK, (q + 1) * BLOCK)
                level_pot = jnp.concatenate(
                    [jnp.broadcast_to(local[:, i:i + 1], (nz, 2 * LANES))
                     for i in range(q * per_block, (q + 1) * per_block)], axis=0)
                value = base[at, :] + jnp.where(diagonal, level_pot * (1.0 / HALF_SPAN), 0.0)
                high = value.astype(BF16).astype(F32)
                tail = jnp.concatenate([turned[at, :]] * 2, axis=1)
                B[p, at, :] = jnp.where(
                    lane < window, high, jnp.where(lane < 2 * window, value - high, tail)).astype(BF16)

    def prepare(v, cs):
        for h in range(2):
            r = nz + h * half
            v[0, r:r + half, cs] = jnp.dot(shifts[0], v[n, r:r + half, cs], preferred_element_type=F32).astype(BF16)
            v[n + 1, r:r + half, cs] = jnp.dot(shifts[1], v[1, r:r + half, cs], preferred_element_type=F32).astype(BF16)

        @pl.loop(0, n, unroll=4)
        def _(p):
            CO[p] = jnp.dot(W[p], v[p + 1, nz:nz + plane, cs], preferred_element_type=F32)

        @pl.loop(0, n, unroll=4)
        def _(p):
            after = lax.rem(p + 1, n)
            rest = widen(EB[p], chunk) * (CO[p, 0:atoms, :] + CO[after, atoms:2 * atoms, :])
            for term in range(2):
                part = rest.astype(BF16)
                rest = rest - part.astype(F32)
                r = term * 2 * atoms
                SP[p, r:r + atoms, :] = part
                SP[after, r + atoms:r + 2 * atoms, :] = part

    def operate(v, cs, finish):
        prepare(v, cs)

        @pl.loop(0, n)
        def _(p):
            terms = SP[p]
            for q in range(plane // BLOCK):
                r = nz + q * BLOCK
                near_rows = v[p + 1, r - nz:r + BLOCK + nz, cs]
                total = jnp.dot(B[p, q * BLOCK:(q + 1) * BLOCK, :],
                                jnp.concatenate([near_rows, near_rows, terms], axis=0),
                                preferred_element_type=F32)
                for k in range(per_block):
                    i = q * per_block + k
                    at = r + k * nz
                    sides = v[p + 2, at:at + nz, cs].astype(F32) + v[p, at:at + nz, cs].astype(F32)
                    weight = -0.5 * (nr / (nr + i)) ** 2 / HALF_SPAN
                    finish(p, at, total[k * nz:(k + 1) * nz] + weight * sides)

    def chunk_lanes(c):
        return slice(c * chunk, (c + 1) * chunk)

    def stage_first(c):
        def finish(p, r, value):
            A[p + 1, r:r + nz, :] = value.astype(BF16)

        operate(O, chunk_lanes(c), finish)

    def stage_filtered(c):
        cs = chunk_lanes(c)

        def finish(p, r, value):
            F[p + 1, r:r + nz, cs] = (2.0 * value - O[p + 1, r:r + nz, cs].astype(F32)).astype(BF16)

        operate(A, slice(0, chunk), finish)

    def stage_image(c):
        cs = chunk_lanes(c)

        def finish(p, r, value):
            I[p, r - nz:r, cs] = (HALF_SPAN * value + CENTER * F[p + 1, r:r + nz, cs].astype(F32)).astype(BF16)

        operate(F, cs, finish)

    part = n // 2
    cuts = 2
    run = part // cuts

    def panel_at(j, u, side, which):
        lane = pl.multiple_of((j + side * pieces) * LANES, LANES)
        return PB.at[pl.ds(which * part + u * run, run), :, pl.ds(lane, LANES)]

    def panel_out(j, u, d):
        to = lax.rem(b + d, nb)
        which = lax.rem(to, 2)
        return remote(F.at[pl.ds(1 + which * part + u * run, run), pl.ds(nz, plane), pl.ds(j * LANES, LANES)],
                      panel_at(j, u, x, which), ps.at[0, j, u, d], pr.at[0, j, u], band=to)

    def panel_cross(j, u, side):
        ref = panel_at(j, u, side, core)
        return remote(ref, ref, ps.at[1, j, u, 0], pr.at[1, j, u], sector=partner)

    def panel_pair(j, u, side, which, own):
        k = 2 if own else 3
        ref = panel_at(j, u, side, which)
        return remote(ref, ref, ps.at[k, j, u, 0], pr.at[k, j, u], band=sibling)

    def when_own(f):
        if both:
            f()
        else:
            pl.when(x == 0)(f)

    def when_other(f):
        if both:
            f()
        else:
            pl.when(x == 1)(f)

    def panel_one(j):
        def go():
            @pl.when(b == owner)
            def _():
                for u in range(cuts):
                    for d in range(1, nb):
                        panel_out(j, u, d).start()
                lane = pl.multiple_of((j + x * pieces) * LANES, LANES)

                @pl.loop(0, part)
                def _(p):
                    PB[core * part + p, :, pl.ds(lane, LANES)] = (
                        F[1 + core * part + p, nz:nz + plane, j * LANES:(j + 1) * LANES])
        when_own(go)

    def panel_two(j):
        def go():
            for u in range(cuts):
                @pl.when(b != owner)
                def _():
                    ref = panel_at(j, u, x, core)
                    remote(ref, ref, ps.at[0, j, u, 0], pr.at[0, j, u], band=sibling).wait_recv()
                panel_cross(j, u, x).start()
                panel_pair(j, u, x, core, True).start()
        when_own(go)

    def panel_three(j):
        def go():
            for u in range(cuts):
                panel_cross(j, u, 1 - x).wait_recv()
                panel_pair(j, u, 1 - x, core, False).start()
        when_other(go)

    def panel_ready():
        for j in range(pieces):
            for u in range(cuts):
                when_own(lambda: panel_pair(j, u, x, 1 - core, True).wait_recv())
                when_other(lambda: panel_pair(j, u, 1 - x, 1 - core, False).wait_recv())

        @pl.loop(0, n)
        def _(p):
            PT[p] = PB[p].T

    def panel_done():
        for j in range(pieces):
            for u in range(cuts):
                def own():
                    @pl.when(b == owner)
                    def _():
                        for d in range(1, nb):
                            panel_out(j, u, d).wait_send()
                    panel_cross(j, u, x).wait_send()
                    panel_pair(j, u, x, core, True).wait_send()
                when_own(own)
                when_other(lambda: panel_pair(j, u, 1 - x, core, False).wait_send())

    scale = 1.0 / (plane * n)

    def result_copy(g, k):
        lo, width = batches[g]
        theirs = pl.ds(pl.multiple_of((1 - x) * rows, 8), rows)
        lanes = pl.ds(lo, width)
        src, dst = (PG, RG) if k == 0 else (PH, RH)
        return remote(src.at[theirs, lanes], dst.at[:, lanes], os.at[k, g], orr.at[k, g], sector=partner)

    def write(out, ref, at, g, side):
        lo, width = batches[g]
        for q in range(lo // LANES, (lo + width) // LANES):
            out[:, pl.ds(source_lane(q, side), LANES)] = ref[at, q * LANES:(q + 1) * LANES] * scale

    def project(g, k):
        lo, width = batches[g]
        cs = slice(lo, lo + width)
        total = PG if k == 0 else PH

        def field(p):
            return F[p + 1, nz:nz + plane, cs] if k == 0 else I[p, :, cs]

        total[:, cs] = jnp.dot(PT[0], field(0), preferred_element_type=F32)

        @pl.loop(1, n)
        def _(p):
            total[:, cs] += jnp.dot(PT[p], field(p), preferred_element_type=F32)

        result_copy(g, k).start()
        write(gram if k == 0 else ham, total, pl.ds(pl.multiple_of(x * rows, 8), rows), g, x)

    def collect(g, k):
        result_copy(g, k).wait_recv()
        write(gram if k == 0 else ham, RG if k == 0 else RH, slice(0, rows), g, 1 - x)

    last_piece = (pieces * LANES - 1) // chunk
    projected = 0
    gather(chunks)
    setup()
    for c in range(chunks):
        if c > 0 and c - 1 < pieces:
            panel_two(c - 1)
        if c > 0:
            pump(c, 2)
            pump(c + 1, 1) if c + 1 < chunks else None
        if c > 1 and c - 2 < pieces and c - 2 < last_piece:
            panel_three(c - 2)
        gather(c)
        pump(c + 1, 1) if c + 1 < chunks else None
        send_own(c + 2)
        stage_first(c)
        stage_filtered(c)
        if c < pieces:
            panel_one(c)
        if c == chunks - 1:
            if last_piece == c:
                panel_two(c)
                panel_three(c)
                panel_ready()
            last = len(batches) - 1
            if projected == last:
                project(last, 0)
        elif c > 0:
            pump(c + 1, 2)
        stage_image(c)
        if c == last_piece + 1:
            panel_three(last_piece)
            panel_ready()
        if last_piece < c < chunks - 1:
            while projected < len(batches) and batches[projected][0] + batches[projected][1] <= (c + 1) * chunk:
                project(projected, 0)
                project(projected, 1)
                projected += 1
    for g in range(projected, len(batches)):
        if g < len(batches) - 1:
            project(g, 0)
        project(g, 1)
    for g in range(len(batches)):
        collect(g, 0)
        collect(g, 1)

    def sent(copy):
        copy.wait_send()

    for c in range(chunks + 1):
        cross(c).wait_send()
        send_plane(c, 0, sent)
        send_plane(c, 1, sent)
        for d in range(1, levels - 1):
            for way in range(2):
                @pl.when(has_source(way, d) & has_target(way))
                def _():
                    sent(relay(c, way, d))
    panel_done()
    for g in range(len(batches)):
        result_copy(g, 0).wait_send()
        result_copy(g, 1).wait_send()


def coefficients(nr, nz):
    plane = nr * nz
    window = BLOCK + 2 * nz
    out = np.zeros((plane, 2 * LANES), np.float64)
    for i in range(nr):
        radius = float(nr + i)
        for z in range(nz):
            row = i * nz + z
            first = row // BLOCK * BLOCK - nz
            terms = {}

            def add(ii, zz, value):
                if 0 <= ii < nr:
                    terms[ii * nz + zz] = terms.get(ii * nz + zz, 0.0) + value

            add(i, z, 2.0 + (nr / radius) ** 2 - CENTER)
            add(i, (z + 1) % nz, -0.5)
            add(i, (z - 1) % nz, -0.5)
            add(i + 1, z, -0.5 * (1.0 + 1.0 / (2.0 * radius)))
            add(i - 1, z, -0.5 * (1.0 - 1.0 / (2.0 * radius)))
            for col, value in terms.items():
                out[row, col - first] = value / HALF_SPAN
                out[row, col - first + window] = value / HALF_SPAN
    return out.astype(np.float32)


def shift_matrices(size, nz):
    row = np.arange(size)[:, None]
    col = np.arange(size)[None, :]
    same = row // nz == col // nz
    gap = (col - row) % nz
    return np.stack([same & (gap == nz - TWIST), same & (gap == TWIST)]).astype(np.float32)


def on_device(n, nb, orbitals, potential, near_points, near_values, far_points, far_values, atom_energy):
    _, nr, nz, cols = orbitals.shape
    plane = nr * nz
    atoms = near_points.shape[0]
    mine = cols // 2
    chunk = LANES
    chunks = mine // chunk
    if chunks >= 4:
        batches = [(0, 2 * chunk)] + [(c * chunk, chunk) for c in range(2, chunks)]
    else:
        batches = [(0, mine)]
    rows = PANEL // n
    panel_dev = PANEL // nb
    pieces = max(panel_dev // LANES // 2, 1)
    hops = n // 2 - 1
    tall = plane + 2 * nz
    vmem = pl.BlockSpec(memory_space=pltpu.VMEM)
    dma = pltpu.SemaphoreType.DMA
    return pl.pallas_call(
        functools.partial(kernel, n, nb, nr, nz, chunk, batches),
        out_shape=(jax.ShapeDtypeStruct((rows, cols), F32),) * 2,
        in_specs=[vmem] * 9,
        out_specs=(vmem,) * 2,
        scratch_shapes=[
            pltpu.VMEM((n + 2, tall, mine), BF16),
            pltpu.VMEM((n + 2, tall, chunk), BF16),
            pltpu.VMEM((n + 2, tall, mine), BF16),
            pltpu.VMEM((n, plane, mine), BF16),
            pltpu.VMEM((n, 2 * atoms, LANES), F32),
            pltpu.VMEM((n, 2 * atoms, plane), BF16),
            pltpu.VMEM((n, plane, 2 * LANES), BF16),
            pltpu.VMEM((n, atoms, LANES), F32),
            pltpu.VMEM((n, 2 * atoms, chunk), F32),
            pltpu.VMEM((n, 4 * atoms, chunk), BF16),
            pltpu.VMEM((n, plane, panel_dev), BF16),
            pltpu.VMEM((n, panel_dev, plane), BF16),
            pltpu.VMEM((panel_dev, mine), F32),
            pltpu.VMEM((panel_dev, mine), F32),
            pltpu.VMEM((rows, mine), F32),
            pltpu.VMEM((rows, mine), F32),
            dma((chunks + 1,)),
            dma((chunks + 1,)),
            dma((2, chunks + 1, hops, 2)),
            dma((2, chunks + 1, hops, 2)),
            dma((4, pieces, 2, nb)),
            dma((4, pieces, 2)),
            dma((2, len(batches))),
            dma((2, len(batches))),
        ],
        compiler_params=pltpu.CompilerParams(
            collective_id=0, has_side_effects=True, vmem_limit_bytes=60 * 2 ** 20
        ),
    )(orbitals.reshape(plane, cols), near_points, near_values, far_points, far_values,
      atom_energy.reshape(1, atoms), potential.reshape(nr, nz).T,
      jnp.asarray(coefficients(nr, nz)), jnp.asarray(shift_matrices(plane // 2, nz)).astype(BF16))


def solution(mesh):
    n, nb = mesh.shape["sector"], mesh.shape["band"]
    return jax.shard_map(
        functools.partial(on_device, n, nb),
        mesh=mesh,
        in_specs=(
            P("sector", None, None, "band"),
            P("sector", None, None),
            P("sector", None),
            P("sector", None),
            P("sector", None),
            P("sector", None),
            P("sector"),
        ),
        out_specs=(P("sector", "band"), P("sector", "band")),
        check_vma=False,
    )
```

```python
import functools

import jax
import jax.numpy as jnp
import numpy as np
from jax import lax
from jax.experimental import pallas as pl
from jax.experimental.pallas import tpu as pltpu
from jax.sharding import PartitionSpec as P

MESH = pl.DeviceIdType.MESH
F32 = jnp.float32
BF16 = jnp.bfloat16

TWIST = 3
PANEL = 2048
CENTER = 6.0
HALF_SPAN = 3.0
LANES = 128
BLOCK = 64


def widen(tile, width):
    return jnp.concatenate([tile] * (width // LANES), axis=1) if width > LANES else tile


def kernel(n, nb, nr, nz, chunk, batches, orb, npts, nval, fpts, fval, energy, pot, base, shifts, ham, gram,
           O, A, F, I, BB, W, B, EB, CO, SP, PB, PT, PH, PG, RH, RG,
           xs, xr, zs, zr, ps, pr, os, orr):
    plane, cols = orb.shape
    rows = ham.shape[0]
    atoms, near_sup = npts.shape
    far_sup = fpts.shape[1]
    half = plane // 2
    mine = cols // 2
    chunks = mine // chunk
    levels = n // 2
    panel_dev = PANEL // nb
    panel_blocks = panel_dev // LANES
    pieces = max(panel_blocks // 2, 1)
    both = panel_blocks >= 2
    order = list(range(pieces)) + ([panel_blocks + j for j in range(pieces)] if both else [])
    window = BLOCK + 2 * nz
    per_block = BLOCK // nz
    s = lax.axis_index("sector")
    b = lax.axis_index("band")
    x = lax.rem(s, 2)
    level = s // 2
    partner = s + 1 - 2 * x
    core = lax.rem(b, 2)
    sibling = b + 1 - 2 * core
    owner = level

    def source_lane(j, side):
        return pl.multiple_of((order[j] + side * pieces) * LANES, LANES)

    def remote(src, dst, send, recv, **device):
        return pltpu.make_async_remote_copy(
            src_ref=src, dst_ref=dst, send_sem=send, recv_sem=recv, device_id=device, device_id_type=MESH)

    def target(way):
        return s + 2 if way == 0 else s - 2

    def has_target(way):
        return level + 1 < levels if way == 0 else level >= 1

    def has_source(way, d):
        return level - d >= 0 if way == 0 else level + d < levels

    def source_level(way, d):
        return level - d if way == 0 else level + d

    barrier = pltpu.get_barrier_semaphore()
    pl.semaphore_signal(barrier, inc=1, device_id={"sector": partner}, device_id_type=MESH)
    for way in range(2):
        @pl.when(has_target(way))
        def _():
            pl.semaphore_signal(barrier, inc=1, device_id={"sector": target(way)}, device_id_type=MESH)
    for d in range(1, nb):
        pl.semaphore_signal(barrier, inc=1, device_id={"band": lax.rem(b + d, nb)}, device_id_type=MESH)

    eye = lax.broadcasted_iota(jnp.int32, (atoms, atoms), 0) == lax.broadcasted_iota(jnp.int32, (atoms, atoms), 1)
    column = jnp.sum(jnp.where(eye, jnp.broadcast_to(energy[...], (atoms, atoms)), 0.0), axis=1, keepdims=True)
    BB[s, 0:atoms, :] = jnp.concatenate(
        [npts[...].astype(F32), nval[...].astype(F32), fpts[...].astype(F32), fval[...].astype(F32)], axis=1)
    BB[s, atoms:2 * atoms, :] = jnp.concatenate(
        [pot[...], jnp.broadcast_to(column, (atoms, LANES - nr))], axis=1)
    ends = jnp.where(level == 0, 1, 0) + jnp.where(level == levels - 1, 1, 0)
    pl.semaphore_wait(barrier, nb + 2 - ends)

    per = chunk // LANES

    def place(c, p, count):
        if c == chunks:
            return BB.at[p] if count == 1 else BB.at[pl.ds(p, count)]
        rows_at, lanes_at = pl.ds(nz, plane), pl.ds(c * chunk, chunk)
        return O.at[p + 1, rows_at, lanes_at] if count == 1 else O.at[pl.ds(p + 1, count), rows_at, lanes_at]

    def own_source(c, side):
        return BB.at[s] if c == chunks else orb.at[:, pl.ds(source_lane(c * per, side), chunk)]

    def cross(c):
        return remote(own_source(c, 1 - x), place(c, s, 1), xs.at[c], xr.at[c], sector=partner)

    def cross_wait(c):
        remote(place(c, partner, 1), place(c, partner, 1), xs.at[c], xr.at[c], sector=partner).wait_recv()

    def direct(c, j, way):
        dst = place(c, s if j == 0 else partner, 1)
        return remote(own_source(c, x) if j == 0 else dst, dst,
                      zs.at[way, c, 0, j], zr.at[way, c, 0, j], sector=target(way))

    def relay(c, way, d):
        ref = place(c, 2 * source_level(way, d), 2)
        return remote(ref, ref, zs.at[way, c, d, 0], zr.at[way, c, d, 0], sector=target(way))

    def arrived(c, way, d):
        lv = source_level(way, d)
        if d == 1:
            for j in range(2):
                ref = place(c, 2 * lv + (x if j == 0 else 1 - x), 1)
                remote(ref, ref, zs.at[way, c, 0, j], zr.at[way, c, 0, j], sector=partner).wait_recv()
        else:
            ref = place(c, 2 * lv, 2)
            remote(ref, ref, zs.at[way, c, d - 1, 0], zr.at[way, c, d - 1, 0], sector=partner).wait_recv()

    def send_plane(c, j, act):
        for way in range(2):
            @pl.when(has_target(way))
            def _():
                act(direct(c, j, way))

    pumped = set()

    def pump(c, d):
        if c > chunks or d >= levels - 1 or (c, d) in pumped:
            return
        pumped.add((c, d))
        for way in range(2):
            @pl.when(has_source(way, d) & has_target(way))
            def _():
                arrived(c, way, d)
                relay(c, way, d).start()

    def gather(c):
        for d in range(1, levels):
            pump(c, d)
        for d in range(1, levels):
            for way in range(2):
                here = has_source(way, d)
                if d < levels - 1:
                    here = here & jnp.logical_not(has_target(way))

                @pl.when(here)
                def _():
                    arrived(c, way, d)

    def start(copy):
        copy.start()

    crossed = set()

    def send_own(c):
        if c >= chunks:
            return
        send_plane(c, 0, start)
        cross_wait(c)
        crossed.add(c)
        send_plane(c, 1, start)

    cross(chunks).start()
    for c in range(chunks):
        cross(c).start()
    send_plane(chunks, 0, start)
    send_plane(0, 0, start)
    for j in range(mine // LANES):
        O[s + 1, nz:nz + plane, j * LANES:(j + 1) * LANES] = orb[:, pl.ds(source_lane(j, x), LANES)]
    cross_wait(chunks)
    send_plane(chunks, 1, start)
    cross_wait(0)
    send_plane(0, 1, start)
    send_own(1)

    for ref, width in ((O, mine), (F, mine), (A, chunk)):
        @pl.loop(0, n)
        def _(p):
            ref[p + 1, 0:nz, :] = jnp.zeros((nz, width), BF16)
            ref[p + 1, nz + plane:nz + plane + nz, :] = jnp.zeros((nz, width), BF16)

    def setup():
        lane = lax.broadcasted_iota(jnp.int32, (BLOCK, 2 * LANES), 1)
        row = lax.broadcasted_iota(jnp.int32, (BLOCK, 2 * LANES), 0)
        diagonal = (lane == row + nz) | (lane == row + nz + window)
        ids = lax.broadcasted_iota(jnp.int32, (atoms, plane), 1).astype(F32)

        @pl.loop(0, n)
        def _(p):
            packed = BB[p, 0:atoms, :]

            def dense(at, count):
                total = jnp.zeros((atoms, plane), F32)
                for j in range(count):
                    point = packed[:, at + j:at + j + 1]
                    value = packed[:, at + count + j:at + count + j + 1]
                    total = total + jnp.where(ids == point, value, 0.0)
                return total.astype(BF16).astype(F32)

            near = dense(0, near_sup)
            far = dense(2 * near_sup, far_sup)
            both_parts = jnp.concatenate([near, far], axis=0)
            W[p] = both_parts.astype(BF16)
            turned = jnp.concatenate([both_parts] * (LANES // (2 * atoms)), axis=0).T
            local = BB[p, atoms:2 * atoms, :]
            EB[p] = jnp.broadcast_to(local[:, nr:nr + 1] * (1.0 / HALF_SPAN), (atoms, LANES))
            for q in range(plane // BLOCK):
                at = slice(q * BLOCK, (q + 1) * BLOCK)
                level_pot = jnp.concatenate(
                    [jnp.broadcast_to(local[:, i:i + 1], (nz, 2 * LANES))
                     for i in range(q * per_block, (q + 1) * per_block)], axis=0)
                value = base[at, :] + jnp.where(diagonal, level_pot * (1.0 / HALF_SPAN), 0.0)
                high = value.astype(BF16).astype(F32)
                tail = jnp.concatenate([turned[at, :]] * 2, axis=1)
                B[p, at, :] = jnp.where(
                    lane < window, high, jnp.where(lane < 2 * window, value - high, tail)).astype(BF16)

    def prepare(v, cs):
        for h in range(2):
            r = nz + h * half
            v[0, r:r + half, cs] = jnp.dot(shifts[0], v[n, r:r + half, cs], preferred_element_type=F32).astype(BF16)
            v[n + 1, r:r + half, cs] = jnp.dot(shifts[1], v[1, r:r + half, cs], preferred_element_type=F32).astype(BF16)

        @pl.loop(0, n, unroll=8)
        def _(p):
            CO[p] = jnp.dot(W[p], v[p + 1, nz:nz + plane, cs], preferred_element_type=F32)

        @pl.loop(0, n, unroll=8)
        def _(p):
            after = lax.rem(p + 1, n)
            rest = widen(EB[p], chunk) * (CO[p, 0:atoms, :] + CO[after, atoms:2 * atoms, :])
            for term in range(2):
                part = rest.astype(BF16)
                rest = rest - part.astype(F32)
                r = term * 2 * atoms
                SP[p, r:r + atoms, :] = part
                SP[after, r + atoms:r + 2 * atoms, :] = part

    def operate(v, cs, finish):
        prepare(v, cs)

        @pl.loop(0, n, unroll=4)
        def _(p):
            terms = SP[p]
            for q in range(plane // BLOCK):
                r = nz + q * BLOCK
                near_rows = v[p + 1, r - nz:r + BLOCK + nz, cs]
                total = jnp.dot(B[p, q * BLOCK:(q + 1) * BLOCK, :],
                                jnp.concatenate([near_rows, near_rows, terms], axis=0),
                                preferred_element_type=F32)
                for k in range(per_block):
                    i = q * per_block + k
                    at = r + k * nz
                    sides = v[p + 2, at:at + nz, cs].astype(F32) + v[p, at:at + nz, cs].astype(F32)
                    weight = -0.5 * (nr / (nr + i)) ** 2 / HALF_SPAN
                    finish(p, at, total[k * nz:(k + 1) * nz] + weight * sides)

    def chunk_lanes(c):
        return slice(c * chunk, (c + 1) * chunk)

    def stage_first(c):
        def finish(p, r, value):
            A[p + 1, r:r + nz, :] = value.astype(BF16)

        operate(O, chunk_lanes(c), finish)

    def stage_filtered(c):
        cs = chunk_lanes(c)

        def finish(p, r, value):
            F[p + 1, r:r + nz, cs] = (2.0 * value - O[p + 1, r:r + nz, cs].astype(F32)).astype(BF16)

        operate(A, slice(0, chunk), finish)

    def stage_image(c):
        cs = chunk_lanes(c)

        def finish(p, r, value):
            I[p, r - nz:r, cs] = (HALF_SPAN * value + CENTER * F[p + 1, r:r + nz, cs].astype(F32)).astype(BF16)

        operate(F, cs, finish)

    part = n // 2
    cuts = 2
    run = part // cuts

    def panel_at(j, u, side, which):
        lane = pl.multiple_of((j + side * pieces) * LANES, LANES)
        return PB.at[pl.ds(which * part + u * run, run), :, pl.ds(lane, LANES)]

    def panel_out(j, u, d):
        to = lax.rem(b + d, nb)
        which = lax.rem(to, 2)
        return remote(F.at[pl.ds(1 + which * part + u * run, run), pl.ds(nz, plane), pl.ds(j * LANES, LANES)],
                      panel_at(j, u, x, which), ps.at[0, j, u, d], pr.at[0, j, u], band=to)

    def panel_cross(j, u, side):
        ref = panel_at(j, u, side, core)
        return remote(ref, ref, ps.at[1, j, u, 0], pr.at[1, j, u], sector=partner)

    def panel_pair(j, u, side, which, own):
        k = 2 if own else 3
        ref = panel_at(j, u, side, which)
        return remote(ref, ref, ps.at[k, j, u, 0], pr.at[k, j, u], band=sibling)

    def when_own(f):
        if both:
            f()
        else:
            pl.when(x == 0)(f)

    def when_other(f):
        if both:
            f()
        else:
            pl.when(x == 1)(f)

    def panel_one(j):
        def go():
            @pl.when(b == owner)
            def _():
                for u in range(cuts):
                    for d in range(1, nb):
                        panel_out(j, u, d).start()
                lane = pl.multiple_of((j + x * pieces) * LANES, LANES)

                @pl.loop(0, part)
                def _(p):
                    PB[core * part + p, :, pl.ds(lane, LANES)] = (
                        F[1 + core * part + p, nz:nz + plane, j * LANES:(j + 1) * LANES])
        when_own(go)

    def panel_two(j):
        def go():
            for u in range(cuts):
                @pl.when(b != owner)
                def _():
                    ref = panel_at(j, u, x, core)
                    remote(ref, ref, ps.at[0, j, u, 0], pr.at[0, j, u], band=sibling).wait_recv()
                panel_cross(j, u, x).start()
                panel_pair(j, u, x, core, True).start()
        when_own(go)

    def panel_three(j):
        def go():
            for u in range(cuts):
                panel_cross(j, u, 1 - x).wait_recv()
                panel_pair(j, u, 1 - x, core, False).start()
        when_other(go)

    def panel_ready():
        for j in range(pieces):
            for u in range(cuts):
                when_own(lambda: panel_pair(j, u, x, 1 - core, True).wait_recv())
                when_other(lambda: panel_pair(j, u, 1 - x, 1 - core, False).wait_recv())

        @pl.loop(0, n)
        def _(p):
            PT[p] = PB[p].T

    def panel_done():
        for j in range(pieces):
            for u in range(cuts):
                def own():
                    @pl.when(b == owner)
                    def _():
                        for d in range(1, nb):
                            panel_out(j, u, d).wait_send()
                    panel_cross(j, u, x).wait_send()
                    panel_pair(j, u, x, core, True).wait_send()
                when_own(own)
                when_other(lambda: panel_pair(j, u, 1 - x, core, False).wait_send())

    scale = 1.0 / (plane * n)

    def result_copy(g, k):
        lo, width = batches[g]
        theirs = pl.ds(pl.multiple_of((1 - x) * rows, 8), rows)
        lanes = pl.ds(lo, width)
        src, dst = (PG, RG) if k == 0 else (PH, RH)
        return remote(src.at[theirs, lanes], dst.at[:, lanes], os.at[k, g], orr.at[k, g], sector=partner)

    def write(out, ref, at, g, side):
        lo, width = batches[g]
        for q in range(lo // LANES, (lo + width) // LANES):
            out[:, pl.ds(source_lane(q, side), LANES)] = ref[at, q * LANES:(q + 1) * LANES] * scale

    def project(g, k):
        lo, width = batches[g]
        cs = slice(lo, lo + width)
        total = PG if k == 0 else PH

        def field(p):
            return F[p + 1, nz:nz + plane, cs] if k == 0 else I[p, :, cs]

        step = min(2 * LANES, panel_dev)
        for m in range(panel_dev // step):
            ms = slice(m * step, (m + 1) * step)
            value = jnp.dot(PT[0, ms, :], field(0), preferred_element_type=F32)
            for p in range(1, n):
                value = value + jnp.dot(PT[p, ms, :], field(p), preferred_element_type=F32)
            total[ms, cs] = value

        result_copy(g, k).start()
        write(gram if k == 0 else ham, total, pl.ds(pl.multiple_of(x * rows, 8), rows), g, x)

    def collect(g, k):
        result_copy(g, k).wait_recv()
        write(gram if k == 0 else ham, RG if k == 0 else RH, slice(0, rows), g, 1 - x)

    last_piece = (pieces * LANES - 1) // chunk
    projected = 0
    gather(chunks)
    setup()
    for c in range(chunks):
        if c > 0 and c - 1 < pieces:
            panel_two(c - 1)
        if c > 0:
            pump(c, 2)
            pump(c + 1, 1) if c + 1 < chunks else None
        if c > 1 and c - 2 < pieces and c - 2 < last_piece:
            panel_three(c - 2)
        gather(c)
        pump(c + 1, 1) if c + 1 < chunks else None
        send_own(c + 2)
        stage_first(c)
        stage_filtered(c)
        if c < pieces:
            panel_one(c)
        if c == chunks - 1:
            if last_piece == c:
                panel_two(c)
                panel_three(c)
                panel_ready()
            last = len(batches) - 1
            if projected == last:
                project(last, 0)
        elif c > 0:
            pump(c + 1, 2)
        stage_image(c)
        if c == last_piece + 1:
            panel_three(last_piece)
            panel_ready()
        if last_piece < c < chunks - 1:
            while projected < len(batches) and batches[projected][0] + batches[projected][1] <= (c + 1) * chunk:
                project(projected, 0)
                project(projected, 1)
                projected += 1
    for g in range(projected, len(batches)):
        if g < len(batches) - 1:
            project(g, 0)
        project(g, 1)
    for g in range(len(batches)):
        collect(g, 0)
        collect(g, 1)

    def sent(copy):
        copy.wait_send()

    for c in range(chunks + 1):
        cross(c).wait_send()
        send_plane(c, 0, sent)
        send_plane(c, 1, sent)
        for d in range(1, levels - 1):
            for way in range(2):
                @pl.when(has_source(way, d) & has_target(way))
                def _():
                    sent(relay(c, way, d))
    panel_done()
    for g in range(len(batches)):
        result_copy(g, 0).wait_send()
        result_copy(g, 1).wait_send()


def coefficients(nr, nz):
    plane = nr * nz
    window = BLOCK + 2 * nz
    out = np.zeros((plane, 2 * LANES), np.float64)
    for i in range(nr):
        radius = float(nr + i)
        for z in range(nz):
            row = i * nz + z
            first = row // BLOCK * BLOCK - nz
            terms = {}

            def add(ii, zz, value):
                if 0 <= ii < nr:
                    terms[ii * nz + zz] = terms.get(ii * nz + zz, 0.0) + value

            add(i, z, 2.0 + (nr / radius) ** 2 - CENTER)
            add(i, (z + 1) % nz, -0.5)
            add(i, (z - 1) % nz, -0.5)
            add(i + 1, z, -0.5 * (1.0 + 1.0 / (2.0 * radius)))
            add(i - 1, z, -0.5 * (1.0 - 1.0 / (2.0 * radius)))
            for col, value in terms.items():
                out[row, col - first] = value / HALF_SPAN
                out[row, col - first + window] = value / HALF_SPAN
    return out.astype(np.float32)


def shift_matrices(size, nz):
    row = np.arange(size)[:, None]
    col = np.arange(size)[None, :]
    same = row // nz == col // nz
    gap = (col - row) % nz
    return np.stack([same & (gap == nz - TWIST), same & (gap == TWIST)]).astype(np.float32)


def on_device(n, nb, orbitals, potential, near_points, near_values, far_points, far_values, atom_energy):
    _, nr, nz, cols = orbitals.shape
    plane = nr * nz
    atoms = near_points.shape[0]
    mine = cols // 2
    chunk = LANES
    chunks = mine // chunk
    if chunks >= 4:
        batches = [(0, 2 * chunk)] + [(c * chunk, chunk) for c in range(2, chunks)]
    else:
        batches = [(0, mine)]
    rows = PANEL // n
    panel_dev = PANEL // nb
    pieces = max(panel_dev // LANES // 2, 1)
    hops = n // 2 - 1
    tall = plane + 2 * nz
    vmem = pl.BlockSpec(memory_space=pltpu.VMEM)
    dma = pltpu.SemaphoreType.DMA
    return pl.pallas_call(
        functools.partial(kernel, n, nb, nr, nz, chunk, batches),
        out_shape=(jax.ShapeDtypeStruct((rows, cols), F32),) * 2,
        in_specs=[vmem] * 9,
        out_specs=(vmem,) * 2,
        scratch_shapes=[
            pltpu.VMEM((n + 2, tall, mine), BF16),
            pltpu.VMEM((n + 2, tall, chunk), BF16),
            pltpu.VMEM((n + 2, tall, mine), BF16),
            pltpu.VMEM((n, plane, mine), BF16),
            pltpu.VMEM((n, 2 * atoms, LANES), F32),
            pltpu.VMEM((n, 2 * atoms, plane), BF16),
            pltpu.VMEM((n, plane, 2 * LANES), BF16),
            pltpu.VMEM((n, atoms, LANES), F32),
            pltpu.VMEM((n, 2 * atoms, chunk), F32),
            pltpu.VMEM((n, 4 * atoms, chunk), BF16),
            pltpu.VMEM((n, plane, panel_dev), BF16),
            pltpu.VMEM((n, panel_dev, plane), BF16),
            pltpu.VMEM((panel_dev, mine), F32),
            pltpu.VMEM((panel_dev, mine), F32),
            pltpu.VMEM((rows, mine), F32),
            pltpu.VMEM((rows, mine), F32),
            dma((chunks + 1,)),
            dma((chunks + 1,)),
            dma((2, chunks + 1, hops, 2)),
            dma((2, chunks + 1, hops, 2)),
            dma((4, pieces, 2, nb)),
            dma((4, pieces, 2)),
            dma((2, len(batches))),
            dma((2, len(batches))),
        ],
        compiler_params=pltpu.CompilerParams(
            collective_id=0, has_side_effects=True, vmem_limit_bytes=60 * 2 ** 20
        ),
    )(orbitals.reshape(plane, cols), near_points, near_values, far_points, far_values,
      atom_energy.reshape(1, atoms), potential.reshape(nr, nz).T,
      jnp.asarray(coefficients(nr, nz)), jnp.asarray(shift_matrices(plane // 2, nz)).astype(BF16))


def solution(mesh):
    n, nb = mesh.shape["sector"], mesh.shape["band"]
    return jax.shard_map(
        functools.partial(on_device, n, nb),
        mesh=mesh,
        in_specs=(
            P("sector", None, None, "band"),
            P("sector", None, None),
            P("sector", None),
            P("sector", None),
            P("sector", None),
            P("sector", None),
            P("sector"),
        ),
        out_specs=(P("sector", "band"), P("sector", "band")),
        check_vma=False,
    )
```

```python
import functools

import jax
import jax.numpy as jnp
import numpy as np
from jax import lax
from jax.experimental import pallas as pl
from jax.experimental.pallas import tpu as pltpu
from jax.sharding import PartitionSpec as P

MESH = pl.DeviceIdType.MESH
F32 = jnp.float32
BF16 = jnp.bfloat16

TWIST = 3
PANEL = 2048
CENTER = 6.0
HALF_SPAN = 3.0
LANES = 128
BLOCK = 64
CUTS = 4


def widen(tile, width):
    return jnp.concatenate([tile] * (width // LANES), axis=1) if width > LANES else tile


def kernel(n, nb, nr, nz, chunk, batches, orb, npts, nval, fpts, fval, energy, pot, base, shifts, ham, gram,
           O, A, F, I, BB, W, B, EB, CO, SP, PB, PT, PH, PG, RH, RG,
           xs, xr, zs, zr, ps, pr, os, orr):
    plane, cols = orb.shape
    rows = ham.shape[0]
    atoms, near_sup = npts.shape
    far_sup = fpts.shape[1]
    half = plane // 2
    mine = cols // 2
    chunks = mine // chunk
    levels = n // 2
    panel_dev = PANEL // nb
    panel_blocks = panel_dev // LANES
    pieces = max(panel_blocks // 2, 1)
    both = panel_blocks >= 2
    order = list(range(pieces)) + ([panel_blocks + j for j in range(pieces)] if both else [])
    window = BLOCK + 2 * nz
    per_block = BLOCK // nz
    s = lax.axis_index("sector")
    b = lax.axis_index("band")
    x = lax.rem(s, 2)
    level = s // 2
    partner = s + 1 - 2 * x
    core = lax.rem(b, 2)
    sibling = b + 1 - 2 * core
    owner = level

    def source_lane(j, side):
        return pl.multiple_of((order[j] + side * pieces) * LANES, LANES)

    def remote(src, dst, send, recv, **device):
        return pltpu.make_async_remote_copy(
            src_ref=src, dst_ref=dst, send_sem=send, recv_sem=recv, device_id=device, device_id_type=MESH)

    def target(way):
        return s + 2 if way == 0 else s - 2

    def has_target(way):
        return level + 1 < levels if way == 0 else level >= 1

    def has_source(way, d):
        return level - d >= 0 if way == 0 else level + d < levels

    def source_level(way, d):
        return level - d if way == 0 else level + d

    barrier = pltpu.get_barrier_semaphore()
    pl.semaphore_signal(barrier, inc=1, device_id={"sector": partner}, device_id_type=MESH)
    for way in range(2):
        @pl.when(has_target(way))
        def _():
            pl.semaphore_signal(barrier, inc=1, device_id={"sector": target(way)}, device_id_type=MESH)
    for d in range(1, nb):
        pl.semaphore_signal(barrier, inc=1, device_id={"band": lax.rem(b + d, nb)}, device_id_type=MESH)

    eye = lax.broadcasted_iota(jnp.int32, (atoms, atoms), 0) == lax.broadcasted_iota(jnp.int32, (atoms, atoms), 1)
    column = jnp.sum(jnp.where(eye, jnp.broadcast_to(energy[...], (atoms, atoms)), 0.0), axis=1, keepdims=True)
    BB[s, 0:atoms, :] = jnp.concatenate(
        [npts[...].astype(F32), nval[...].astype(F32), fpts[...].astype(F32), fval[...].astype(F32)], axis=1)
    BB[s, atoms:2 * atoms, :] = jnp.concatenate(
        [pot[...], jnp.broadcast_to(column, (atoms, LANES - nr))], axis=1)
    ends = jnp.where(level == 0, 1, 0) + jnp.where(level == levels - 1, 1, 0)
    pl.semaphore_wait(barrier, nb + 2 - ends)

    per = chunk // LANES

    def place(c, p, count):
        if c == chunks:
            return BB.at[p] if count == 1 else BB.at[pl.ds(p, count)]
        rows_at, lanes_at = pl.ds(nz, plane), pl.ds(c * chunk, chunk)
        return O.at[p + 1, rows_at, lanes_at] if count == 1 else O.at[pl.ds(p + 1, count), rows_at, lanes_at]

    def own_source(c, side):
        return BB.at[s] if c == chunks else orb.at[:, pl.ds(source_lane(c * per, side), chunk)]

    def cross(c):
        return remote(own_source(c, 1 - x), place(c, s, 1), xs.at[c], xr.at[c], sector=partner)

    def cross_wait(c):
        remote(place(c, partner, 1), place(c, partner, 1), xs.at[c], xr.at[c], sector=partner).wait_recv()

    def direct(c, j, way):
        dst = place(c, s if j == 0 else partner, 1)
        return remote(own_source(c, x) if j == 0 else dst, dst,
                      zs.at[way, c, 0, j], zr.at[way, c, 0, j], sector=target(way))

    def relay(c, way, d):
        ref = place(c, 2 * source_level(way, d), 2)
        return remote(ref, ref, zs.at[way, c, d, 0], zr.at[way, c, d, 0], sector=target(way))

    def arrived(c, way, d):
        lv = source_level(way, d)
        if d == 1:
            for j in range(2):
                ref = place(c, 2 * lv + (x if j == 0 else 1 - x), 1)
                remote(ref, ref, zs.at[way, c, 0, j], zr.at[way, c, 0, j], sector=partner).wait_recv()
        else:
            ref = place(c, 2 * lv, 2)
            remote(ref, ref, zs.at[way, c, d - 1, 0], zr.at[way, c, d - 1, 0], sector=partner).wait_recv()

    def send_plane(c, j, act):
        for way in range(2):
            @pl.when(has_target(way))
            def _():
                act(direct(c, j, way))

    pumped = set()

    def pump(c, d):
        if c > chunks or d >= levels - 1 or (c, d) in pumped:
            return
        pumped.add((c, d))
        for way in range(2):
            @pl.when(has_source(way, d) & has_target(way))
            def _():
                arrived(c, way, d)
                relay(c, way, d).start()

    def gather(c):
        for d in range(1, levels):
            pump(c, d)
        for d in range(1, levels):
            for way in range(2):
                here = has_source(way, d)
                if d < levels - 1:
                    here = here & jnp.logical_not(has_target(way))

                @pl.when(here)
                def _():
                    arrived(c, way, d)

    def start(copy):
        copy.start()

    crossed = set()

    def send_own(c):
        if c >= chunks:
            return
        send_plane(c, 0, start)
        cross_wait(c)
        crossed.add(c)
        send_plane(c, 1, start)

    cross(chunks).start()
    for c in range(chunks):
        cross(c).start()
    send_plane(chunks, 0, start)
    send_plane(0, 0, start)
    for j in range(mine // LANES):
        O[s + 1, nz:nz + plane, j * LANES:(j + 1) * LANES] = orb[:, pl.ds(source_lane(j, x), LANES)]
    cross_wait(chunks)
    send_plane(chunks, 1, start)
    cross_wait(0)
    send_plane(0, 1, start)
    send_own(1)

    for ref, width in ((O, mine), (F, mine), (A, chunk)):
        @pl.loop(0, n)
        def _(p):
            ref[p + 1, 0:nz, :] = jnp.zeros((nz, width), BF16)
            ref[p + 1, nz + plane:nz + plane + nz, :] = jnp.zeros((nz, width), BF16)

    def setup():
        lane = lax.broadcasted_iota(jnp.int32, (BLOCK, 2 * LANES), 1)
        row = lax.broadcasted_iota(jnp.int32, (BLOCK, 2 * LANES), 0)
        diagonal = (lane == row + nz) | (lane == row + nz + window)
        ids = lax.broadcasted_iota(jnp.int32, (atoms, plane), 1).astype(F32)

        @pl.loop(0, n)
        def _(p):
            packed = BB[p, 0:atoms, :]

            def dense(at, count):
                total = jnp.zeros((atoms, plane), F32)
                for j in range(count):
                    point = packed[:, at + j:at + j + 1]
                    value = packed[:, at + count + j:at + count + j + 1]
                    total = total + jnp.where(ids == point, value, 0.0)
                return total.astype(BF16).astype(F32)

            near = dense(0, near_sup)
            far = dense(2 * near_sup, far_sup)
            both_parts = jnp.concatenate([near, far], axis=0)
            W[p] = both_parts.astype(BF16)
            turned = jnp.concatenate([both_parts] * (LANES // (2 * atoms)), axis=0).T
            local = BB[p, atoms:2 * atoms, :]
            EB[p] = jnp.broadcast_to(local[:, nr:nr + 1] * (1.0 / HALF_SPAN), (atoms, LANES))
            for q in range(plane // BLOCK):
                at = slice(q * BLOCK, (q + 1) * BLOCK)
                level_pot = jnp.concatenate(
                    [jnp.broadcast_to(local[:, i:i + 1], (nz, 2 * LANES))
                     for i in range(q * per_block, (q + 1) * per_block)], axis=0)
                value = base[at, :] + jnp.where(diagonal, level_pot * (1.0 / HALF_SPAN), 0.0)
                high = value.astype(BF16).astype(F32)
                tail = jnp.concatenate([turned[at, :]] * 2, axis=1)
                B[p, at, :] = jnp.where(
                    lane < window, high, jnp.where(lane < 2 * window, value - high, tail)).astype(BF16)

    def prepare(v, cs):
        for h in range(2):
            r = nz + h * half
            v[0, r:r + half, cs] = jnp.dot(shifts[0], v[n, r:r + half, cs], preferred_element_type=F32).astype(BF16)
            v[n + 1, r:r + half, cs] = jnp.dot(shifts[1], v[1, r:r + half, cs], preferred_element_type=F32).astype(BF16)

        @pl.loop(0, n, unroll=8)
        def _(p):
            CO[p] = jnp.dot(W[p], v[p + 1, nz:nz + plane, cs], preferred_element_type=F32)

        @pl.loop(0, n, unroll=8)
        def _(p):
            after = lax.rem(p + 1, n)
            rest = widen(EB[p], chunk) * (CO[p, 0:atoms, :] + CO[after, atoms:2 * atoms, :])
            for term in range(2):
                part = rest.astype(BF16)
                rest = rest - part.astype(F32)
                r = term * 2 * atoms
                SP[p, r:r + atoms, :] = part
                SP[after, r + atoms:r + 2 * atoms, :] = part

    def operate(v, cs, finish):
        prepare(v, cs)

        @pl.loop(0, n, unroll=4)
        def _(p):
            terms = SP[p]
            for q in range(plane // BLOCK):
                r = nz + q * BLOCK
                near_rows = v[p + 1, r - nz:r + BLOCK + nz, cs]
                total = jnp.dot(B[p, q * BLOCK:(q + 1) * BLOCK, :],
                                jnp.concatenate([near_rows, near_rows, terms], axis=0),
                                preferred_element_type=F32)
                for k in range(per_block):
                    i = q * per_block + k
                    at = r + k * nz
                    sides = v[p + 2, at:at + nz, cs].astype(F32) + v[p, at:at + nz, cs].astype(F32)
                    weight = -0.5 * (nr / (nr + i)) ** 2 / HALF_SPAN
                    finish(p, at, total[k * nz:(k + 1) * nz] + weight * sides)

    def chunk_lanes(c):
        return slice(c * chunk, (c + 1) * chunk)

    def stage_first(c):
        def finish(p, r, value):
            A[p + 1, r:r + nz, :] = value.astype(BF16)

        operate(O, chunk_lanes(c), finish)

    def stage_filtered(c):
        cs = chunk_lanes(c)

        def finish(p, r, value):
            F[p + 1, r:r + nz, cs] = (2.0 * value - O[p + 1, r:r + nz, cs].astype(F32)).astype(BF16)

        operate(A, slice(0, chunk), finish)

    def stage_image(c):
        cs = chunk_lanes(c)

        def finish(p, r, value):
            I[p, r - nz:r, cs] = (HALF_SPAN * value + CENTER * F[p + 1, r:r + nz, cs].astype(F32)).astype(BF16)

        operate(F, cs, finish)

    part = n // 2
    cuts = CUTS
    run = part // cuts

    def panel_at(j, u, side, which):
        lane = pl.multiple_of((j + side * pieces) * LANES, LANES)
        return PB.at[pl.ds(which * part + u * run, run), :, pl.ds(lane, LANES)]

    def panel_out(j, u, d):
        to = lax.rem(b + d, nb)
        which = lax.rem(to, 2)
        return remote(F.at[pl.ds(1 + which * part + u * run, run), pl.ds(nz, plane), pl.ds(j * LANES, LANES)],
                      panel_at(j, u, x, which), ps.at[0, j, u, d], pr.at[0, j, u], band=to)

    def panel_cross(j, u, side):
        ref = panel_at(j, u, side, core)
        return remote(ref, ref, ps.at[1, j, u, 0], pr.at[1, j, u], sector=partner)

    def panel_pair(j, u, side, which, own):
        k = 2 if own else 3
        ref = panel_at(j, u, side, which)
        return remote(ref, ref, ps.at[k, j, u, 0], pr.at[k, j, u], band=sibling)

    def when_own(f):
        if both:
            f()
        else:
            pl.when(x == 0)(f)

    def when_other(f):
        if both:
            f()
        else:
            pl.when(x == 1)(f)

    def panel_one(j):
        def go():
            @pl.when(b == owner)
            def _():
                for u in range(cuts):
                    for d in range(1, nb):
                        panel_out(j, u, d).start()
                lane = pl.multiple_of((j + x * pieces) * LANES, LANES)

                @pl.loop(0, part)
                def _(p):
                    PB[core * part + p, :, pl.ds(lane, LANES)] = (
                        F[1 + core * part + p, nz:nz + plane, j * LANES:(j + 1) * LANES])
        when_own(go)

    def panel_two(j):
        def go():
            for u in range(cuts):
                @pl.when(b != owner)
                def _():
                    ref = panel_at(j, u, x, core)
                    remote(ref, ref, ps.at[0, j, u, 0], pr.at[0, j, u], band=sibling).wait_recv()
                panel_cross(j, u, x).start()
                panel_pair(j, u, x, core, True).start()
        when_own(go)

    def panel_three(j):
        def go():
            for u in range(cuts):
                panel_cross(j, u, 1 - x).wait_recv()
                panel_pair(j, u, 1 - x, core, False).start()
        when_other(go)

    def panel_ready():
        for j in range(pieces):
            for u in range(cuts):
                when_own(lambda: panel_pair(j, u, x, 1 - core, True).wait_recv())
                when_other(lambda: panel_pair(j, u, 1 - x, 1 - core, False).wait_recv())

        @pl.loop(0, n)
        def _(p):
            PT[p] = PB[p].T

    def panel_done():
        for j in range(pieces):
            for u in range(cuts):
                def own():
                    @pl.when(b == owner)
                    def _():
                        for d in range(1, nb):
                            panel_out(j, u, d).wait_send()
                    panel_cross(j, u, x).wait_send()
                    panel_pair(j, u, x, core, True).wait_send()
                when_own(own)
                when_other(lambda: panel_pair(j, u, 1 - x, core, False).wait_send())

    scale = 1.0 / (plane * n)

    def result_copy(g, k):
        lo, width = batches[g]
        theirs = pl.ds(pl.multiple_of((1 - x) * rows, 8), rows)
        lanes = pl.ds(lo, width)
        src, dst = (PG, RG) if k == 0 else (PH, RH)
        return remote(src.at[theirs, lanes], dst.at[:, lanes], os.at[k, g], orr.at[k, g], sector=partner)

    def write(out, ref, at, g, side):
        lo, width = batches[g]
        for q in range(lo // LANES, (lo + width) // LANES):
            out[:, pl.ds(source_lane(q, side), LANES)] = ref[at, q * LANES:(q + 1) * LANES] * scale

    def project(g, k):
        lo, width = batches[g]
        cs = slice(lo, lo + width)
        total = PG if k == 0 else PH

        def field(p):
            return F[p + 1, nz:nz + plane, cs] if k == 0 else I[p, :, cs]

        step = min(2 * LANES, panel_dev)
        for m in range(panel_dev // step):
            ms = slice(m * step, (m + 1) * step)
            value = jnp.dot(PT[0, ms, :], field(0), preferred_element_type=F32)
            for p in range(1, n):
                value = value + jnp.dot(PT[p, ms, :], field(p), preferred_element_type=F32)
            total[ms, cs] = value

        result_copy(g, k).start()
        write(gram if k == 0 else ham, total, pl.ds(pl.multiple_of(x * rows, 8), rows), g, x)

    def collect(g, k):
        result_copy(g, k).wait_recv()
        write(gram if k == 0 else ham, RG if k == 0 else RH, slice(0, rows), g, 1 - x)

    last_piece = (pieces * LANES - 1) // chunk
    projected = 0
    gather(chunks)
    pump(0, 1)
    setup()
    for c in range(chunks):
        gather(c)
        if c + 1 < chunks:
            pump(c + 1, 1)
        stage_first(c)
        stage_filtered(c)
        if c < pieces:
            panel_one(c)
        if c == 0:
            if chunks > 1:
                pump(1, 2)
            for later in range(2, chunks):
                send_own(later)
        if c == chunks - 1:
            if last_piece == c:
                panel_two(c)
                panel_three(c)
                panel_ready()
            last = len(batches) - 1
            if projected == last:
                project(last, 0)
        stage_image(c)
        if c < pieces and c < chunks - 1:
            if c > 0:
                panel_three(c - 1)
                if c + 1 < chunks:
                    pump(c + 1, 2)
                if c + 2 < chunks:
                    pump(c + 2, 1)
            panel_two(c)
            if c == last_piece:
                if c + 2 < chunks:
                    pump(c + 2, 2)
                panel_three(c)
                panel_ready()
        if last_piece <= c < chunks - 1:
            while projected < len(batches) and batches[projected][0] + batches[projected][1] <= (c + 1) * chunk:
                project(projected, 0)
                project(projected, 1)
                projected += 1
    for g in range(projected, len(batches)):
        if g < len(batches) - 1:
            project(g, 0)
        project(g, 1)
    for g in range(len(batches)):
        collect(g, 0)
        collect(g, 1)

    def sent(copy):
        copy.wait_send()

    for c in range(chunks + 1):
        cross(c).wait_send()
        send_plane(c, 0, sent)
        send_plane(c, 1, sent)
        for d in range(1, levels - 1):
            for way in range(2):
                @pl.when(has_source(way, d) & has_target(way))
                def _():
                    sent(relay(c, way, d))
    panel_done()
    for g in range(len(batches)):
        result_copy(g, 0).wait_send()
        result_copy(g, 1).wait_send()


def coefficients(nr, nz):
    plane = nr * nz
    window = BLOCK + 2 * nz
    out = np.zeros((plane, 2 * LANES), np.float64)
    for i in range(nr):
        radius = float(nr + i)
        for z in range(nz):
            row = i * nz + z
            first = row // BLOCK * BLOCK - nz
            terms = {}

            def add(ii, zz, value):
                if 0 <= ii < nr:
                    terms[ii * nz + zz] = terms.get(ii * nz + zz, 0.0) + value

            add(i, z, 2.0 + (nr / radius) ** 2 - CENTER)
            add(i, (z + 1) % nz, -0.5)
            add(i, (z - 1) % nz, -0.5)
            add(i + 1, z, -0.5 * (1.0 + 1.0 / (2.0 * radius)))
            add(i - 1, z, -0.5 * (1.0 - 1.0 / (2.0 * radius)))
            for col, value in terms.items():
                out[row, col - first] = value / HALF_SPAN
                out[row, col - first + window] = value / HALF_SPAN
    return out.astype(np.float32)


def shift_matrices(size, nz):
    row = np.arange(size)[:, None]
    col = np.arange(size)[None, :]
    same = row // nz == col // nz
    gap = (col - row) % nz
    return np.stack([same & (gap == nz - TWIST), same & (gap == TWIST)]).astype(np.float32)


def on_device(n, nb, orbitals, potential, near_points, near_values, far_points, far_values, atom_energy):
    _, nr, nz, cols = orbitals.shape
    plane = nr * nz
    atoms = near_points.shape[0]
    mine = cols // 2
    chunk = LANES
    chunks = mine // chunk
    if chunks >= 4:
        batches = [(0, 2 * chunk)] + [(c * chunk, chunk) for c in range(2, chunks)]
    else:
        batches = [(0, mine)]
    rows = PANEL // n
    panel_dev = PANEL // nb
    pieces = max(panel_dev // LANES // 2, 1)
    hops = n // 2 - 1
    tall = plane + 2 * nz
    vmem = pl.BlockSpec(memory_space=pltpu.VMEM)
    dma = pltpu.SemaphoreType.DMA
    return pl.pallas_call(
        functools.partial(kernel, n, nb, nr, nz, chunk, batches),
        out_shape=(jax.ShapeDtypeStruct((rows, cols), F32),) * 2,
        in_specs=[vmem] * 9,
        out_specs=(vmem,) * 2,
        scratch_shapes=[
            pltpu.VMEM((n + 2, tall, mine), BF16),
            pltpu.VMEM((n + 2, tall, chunk), BF16),
            pltpu.VMEM((n + 2, tall, mine), BF16),
            pltpu.VMEM((n, plane, mine), BF16),
            pltpu.VMEM((n, 2 * atoms, LANES), F32),
            pltpu.VMEM((n, 2 * atoms, plane), BF16),
            pltpu.VMEM((n, plane, 2 * LANES), BF16),
            pltpu.VMEM((n, atoms, LANES), F32),
            pltpu.VMEM((n, 2 * atoms, chunk), F32),
            pltpu.VMEM((n, 4 * atoms, chunk), BF16),
            pltpu.VMEM((n, plane, panel_dev), BF16),
            pltpu.VMEM((n, panel_dev, plane), BF16),
            pltpu.VMEM((panel_dev, mine), F32),
            pltpu.VMEM((panel_dev, mine), F32),
            pltpu.VMEM((rows, mine), F32),
            pltpu.VMEM((rows, mine), F32),
            dma((chunks + 1,)),
            dma((chunks + 1,)),
            dma((2, chunks + 1, hops, 2)),
            dma((2, chunks + 1, hops, 2)),
            dma((4, pieces, CUTS, nb)),
            dma((4, pieces, CUTS)),
            dma((2, len(batches))),
            dma((2, len(batches))),
        ],
        compiler_params=pltpu.CompilerParams(
            collective_id=0, has_side_effects=True, vmem_limit_bytes=60 * 2 ** 20
        ),
    )(orbitals.reshape(plane, cols), near_points, near_values, far_points, far_values,
      atom_energy.reshape(1, atoms), potential.reshape(nr, nz).T,
      jnp.asarray(coefficients(nr, nz)), jnp.asarray(shift_matrices(plane // 2, nz)).astype(BF16))


def solution(mesh):
    n, nb = mesh.shape["sector"], mesh.shape["band"]
    return jax.shard_map(
        functools.partial(on_device, n, nb),
        mesh=mesh,
        in_specs=(
            P("sector", None, None, "band"),
            P("sector", None, None),
            P("sector", None),
            P("sector", None),
            P("sector", None),
            P("sector", None),
            P("sector"),
        ),
        out_specs=(P("sector", "band"), P("sector", "band")),
        check_vma=False,
    )
```

```python
import functools

import jax
import jax.numpy as jnp
import numpy as np
from jax import lax
from jax.experimental import pallas as pl
from jax.experimental.pallas import tpu as pltpu
from jax.sharding import PartitionSpec as P

MESH = pl.DeviceIdType.MESH
F32 = jnp.float32
BF16 = jnp.bfloat16

TWIST = 3
PANEL = 2048
CENTER = 6.0
HALF_SPAN = 3.0
LANES = 128
BLOCK = 64
CUTS = 4


def widen(tile, width):
    return jnp.concatenate([tile] * (width // LANES), axis=1) if width > LANES else tile


def kernel(n, nb, nr, nz, chunk, batches, *refs):
    count = 9
    given, (ham, gram), held = refs[:count], refs[count:count + 2], refs[count + 2:2 * count + 2]
    orb, npts, nval, fpts, fval, energy, pot, base, shifts = held
    (O, A, F, I, BB, W, B, EB, CO, SP, PB, PT, PH, PG, RH, RG,
     xs, xr, zs, zr, ps, pr, os, orr, load) = refs[2 * count + 2:]
    loads = [pltpu.make_async_copy(src, dst, load.at[i]) for i, (src, dst) in enumerate(zip(given, held))]
    for copy in loads[1:7] + loads[:1] + loads[7:]:
        copy.start()
    plane, cols = orb.shape
    rows = ham.shape[0]
    atoms, near_sup = npts.shape
    far_sup = fpts.shape[1]
    half = plane // 2
    mine = cols // 2
    chunks = mine // chunk
    levels = n // 2
    panel_dev = PANEL // nb
    panel_blocks = panel_dev // LANES
    pieces = max(panel_blocks // 2, 1)
    both = panel_blocks >= 2
    order = list(range(pieces)) + ([panel_blocks + j for j in range(pieces)] if both else [])
    window = BLOCK + 2 * nz
    per_block = BLOCK // nz
    s = lax.axis_index("sector")
    b = lax.axis_index("band")
    x = lax.rem(s, 2)
    level = s // 2
    partner = s + 1 - 2 * x
    core = lax.rem(b, 2)
    sibling = b + 1 - 2 * core
    owner = level

    def source_lane(j, side):
        return pl.multiple_of((order[j] + side * pieces) * LANES, LANES)

    def remote(src, dst, send, recv, **device):
        return pltpu.make_async_remote_copy(
            src_ref=src, dst_ref=dst, send_sem=send, recv_sem=recv, device_id=device, device_id_type=MESH)

    def target(way):
        return s + 2 if way == 0 else s - 2

    def has_target(way):
        return level + 1 < levels if way == 0 else level >= 1

    def has_source(way, d):
        return level - d >= 0 if way == 0 else level + d < levels

    def source_level(way, d):
        return level - d if way == 0 else level + d

    barrier = pltpu.get_barrier_semaphore()
    pl.semaphore_signal(barrier, inc=1, device_id={"sector": partner}, device_id_type=MESH)
    for way in range(2):
        @pl.when(has_target(way))
        def _():
            pl.semaphore_signal(barrier, inc=1, device_id={"sector": target(way)}, device_id_type=MESH)
    for d in range(1, nb):
        pl.semaphore_signal(barrier, inc=1, device_id={"band": lax.rem(b + d, nb)}, device_id_type=MESH)

    for copy in loads[1:7]:
        copy.wait()
    eye = lax.broadcasted_iota(jnp.int32, (atoms, atoms), 0) == lax.broadcasted_iota(jnp.int32, (atoms, atoms), 1)
    column = jnp.sum(jnp.where(eye, jnp.broadcast_to(energy[...], (atoms, atoms)), 0.0), axis=1, keepdims=True)
    BB[s, 0:atoms, :] = jnp.concatenate(
        [npts[...].astype(F32), nval[...].astype(F32), fpts[...].astype(F32), fval[...].astype(F32)], axis=1)
    BB[s, atoms:2 * atoms, :] = jnp.concatenate(
        [pot[...], jnp.broadcast_to(column, (atoms, LANES - nr))], axis=1)
    ends = jnp.where(level == 0, 1, 0) + jnp.where(level == levels - 1, 1, 0)
    pl.semaphore_wait(barrier, nb + 2 - ends)

    loads[0].wait()
    per = chunk // LANES

    def place(c, p, count):
        if c == chunks:
            return BB.at[p] if count == 1 else BB.at[pl.ds(p, count)]
        rows_at, lanes_at = pl.ds(nz, plane), pl.ds(c * chunk, chunk)
        return O.at[p + 1, rows_at, lanes_at] if count == 1 else O.at[pl.ds(p + 1, count), rows_at, lanes_at]

    def own_source(c, side):
        return BB.at[s] if c == chunks else orb.at[:, pl.ds(source_lane(c * per, side), chunk)]

    def cross(c):
        return remote(own_source(c, 1 - x), place(c, s, 1), xs.at[c], xr.at[c], sector=partner)

    def cross_wait(c):
        remote(place(c, partner, 1), place(c, partner, 1), xs.at[c], xr.at[c], sector=partner).wait_recv()

    def direct(c, j, way):
        dst = place(c, s if j == 0 else partner, 1)
        return remote(own_source(c, x) if j == 0 else dst, dst,
                      zs.at[way, c, 0, j], zr.at[way, c, 0, j], sector=target(way))

    def relay(c, way, d):
        ref = place(c, 2 * source_level(way, d), 2)
        return remote(ref, ref, zs.at[way, c, d, 0], zr.at[way, c, d, 0], sector=target(way))

    def arrived(c, way, d):
        lv = source_level(way, d)
        if d == 1:
            for j in range(2):
                ref = place(c, 2 * lv + (x if j == 0 else 1 - x), 1)
                remote(ref, ref, zs.at[way, c, 0, j], zr.at[way, c, 0, j], sector=partner).wait_recv()
        else:
            ref = place(c, 2 * lv, 2)
            remote(ref, ref, zs.at[way, c, d - 1, 0], zr.at[way, c, d - 1, 0], sector=partner).wait_recv()

    def send_plane(c, j, act):
        for way in range(2):
            @pl.when(has_target(way))
            def _():
                act(direct(c, j, way))

    pumped = set()

    def pump(c, d):
        if c > chunks or d >= levels - 1 or (c, d) in pumped:
            return
        pumped.add((c, d))
        for way in range(2):
            @pl.when(has_source(way, d) & has_target(way))
            def _():
                arrived(c, way, d)
                relay(c, way, d).start()

    def gather(c):
        for d in range(1, levels):
            pump(c, d)
        for d in range(1, levels):
            for way in range(2):
                here = has_source(way, d)
                if d < levels - 1:
                    here = here & jnp.logical_not(has_target(way))

                @pl.when(here)
                def _():
                    arrived(c, way, d)

    def start(copy):
        copy.start()

    outermost = (level == 0) | (level == levels - 1)

    def send_own(c):
        send_plane(c, 0, start)
        cross_wait(c)
        send_plane(c, 1, start)

    def send_late(c, when):
        @pl.when(when)
        def _():
            send_own(c)

    cross(chunks).start()
    for c in range(chunks):
        cross(c).start()
    send_plane(chunks, 0, start)
    send_plane(0, 0, start)
    for j in range(mine // LANES):
        O[s + 1, nz:nz + plane, j * LANES:(j + 1) * LANES] = orb[:, pl.ds(source_lane(j, x), LANES)]
    cross_wait(chunks)
    send_plane(chunks, 1, start)
    cross_wait(0)
    send_plane(0, 1, start)
    for c in range(1, chunks):
        send_late(c, outermost)

    for ref, width in ((O, mine), (F, mine), (A, chunk)):
        @pl.loop(0, n)
        def _(p):
            ref[p + 1, 0:nz, :] = jnp.zeros((nz, width), BF16)
            ref[p + 1, nz + plane:nz + plane + nz, :] = jnp.zeros((nz, width), BF16)

    def setup():
        lane = lax.broadcasted_iota(jnp.int32, (BLOCK, 2 * LANES), 1)
        row = lax.broadcasted_iota(jnp.int32, (BLOCK, 2 * LANES), 0)
        diagonal = (lane == row + nz) | (lane == row + nz + window)
        ids = lax.broadcasted_iota(jnp.int32, (atoms, plane), 1).astype(F32)

        @pl.loop(0, n)
        def _(p):
            packed = BB[p, 0:atoms, :]

            def dense(at, count):
                total = jnp.zeros((atoms, plane), F32)
                for j in range(count):
                    point = packed[:, at + j:at + j + 1]
                    value = packed[:, at + count + j:at + count + j + 1]
                    total = total + jnp.where(ids == point, value, 0.0)
                return total.astype(BF16).astype(F32)

            near = dense(0, near_sup)
            far = dense(2 * near_sup, far_sup)
            both_parts = jnp.concatenate([near, far], axis=0)
            W[p] = both_parts.astype(BF16)
            turned = jnp.concatenate([both_parts] * (LANES // (2 * atoms)), axis=0).T
            local = BB[p, atoms:2 * atoms, :]
            EB[p] = jnp.broadcast_to(local[:, nr:nr + 1] * (1.0 / HALF_SPAN), (atoms, LANES))
            for q in range(plane // BLOCK):
                at = slice(q * BLOCK, (q + 1) * BLOCK)
                level_pot = jnp.concatenate(
                    [jnp.broadcast_to(local[:, i:i + 1], (nz, 2 * LANES))
                     for i in range(q * per_block, (q + 1) * per_block)], axis=0)
                value = base[at, :] + jnp.where(diagonal, level_pot * (1.0 / HALF_SPAN), 0.0)
                high = value.astype(BF16).astype(F32)
                tail = jnp.concatenate([turned[at, :]] * 2, axis=1)
                B[p, at, :] = jnp.where(
                    lane < window, high, jnp.where(lane < 2 * window, value - high, tail)).astype(BF16)

    def prepare(v, cs):
        for h in range(2):
            r = nz + h * half
            v[0, r:r + half, cs] = jnp.dot(shifts[0], v[n, r:r + half, cs], preferred_element_type=F32).astype(BF16)
            v[n + 1, r:r + half, cs] = jnp.dot(shifts[1], v[1, r:r + half, cs], preferred_element_type=F32).astype(BF16)

        @pl.loop(0, n, unroll=8)
        def _(p):
            CO[p] = jnp.dot(W[p], v[p + 1, nz:nz + plane, cs], preferred_element_type=F32)

        @pl.loop(0, n, unroll=8)
        def _(p):
            after = lax.rem(p + 1, n)
            rest = widen(EB[p], chunk) * (CO[p, 0:atoms, :] + CO[after, atoms:2 * atoms, :])
            for term in range(2):
                part = rest.astype(BF16)
                rest = rest - part.astype(F32)
                r = term * 2 * atoms
                SP[p, r:r + atoms, :] = part
                SP[after, r + atoms:r + 2 * atoms, :] = part

    def operate(v, cs, finish):
        prepare(v, cs)

        @pl.loop(0, n, unroll=4)
        def _(p):
            terms = SP[p]
            for q in range(plane // BLOCK):
                r = nz + q * BLOCK
                near_rows = v[p + 1, r - nz:r + BLOCK + nz, cs]
                total = jnp.dot(B[p, q * BLOCK:(q + 1) * BLOCK, :],
                                jnp.concatenate([near_rows, near_rows, terms], axis=0),
                                preferred_element_type=F32)
                for k in range(per_block):
                    i = q * per_block + k
                    at = r + k * nz
                    sides = v[p + 2, at:at + nz, cs].astype(F32) + v[p, at:at + nz, cs].astype(F32)
                    weight = -0.5 * (nr / (nr + i)) ** 2 / HALF_SPAN
                    finish(p, at, total[k * nz:(k + 1) * nz] + weight * sides)

    def chunk_lanes(c):
        return slice(c * chunk, (c + 1) * chunk)

    def stage_first(c):
        def finish(p, r, value):
            A[p + 1, r:r + nz, :] = value.astype(BF16)

        operate(O, chunk_lanes(c), finish)

    def stage_filtered(c):
        cs = chunk_lanes(c)

        def finish(p, r, value):
            F[p + 1, r:r + nz, cs] = (2.0 * value - O[p + 1, r:r + nz, cs].astype(F32)).astype(BF16)

        operate(A, slice(0, chunk), finish)

    def stage_image(c):
        cs = chunk_lanes(c)

        def finish(p, r, value):
            I[p, r - nz:r, cs] = (HALF_SPAN * value + CENTER * F[p + 1, r:r + nz, cs].astype(F32)).astype(BF16)

        operate(F, cs, finish)

    part = n // 2
    cuts = CUTS
    run = part // cuts

    def panel_at(j, u, side, which):
        lane = pl.multiple_of((j + side * pieces) * LANES, LANES)
        return PB.at[pl.ds(which * part + u * run, run), :, pl.ds(lane, LANES)]

    def panel_out(j, u, d):
        to = lax.rem(b + d, nb)
        which = lax.rem(to, 2)
        return remote(F.at[pl.ds(1 + which * part + u * run, run), pl.ds(nz, plane), pl.ds(j * LANES, LANES)],
                      panel_at(j, u, x, which), ps.at[0, j, u, d], pr.at[0, j, u], band=to)

    def panel_cross(j, u, side):
        ref = panel_at(j, u, side, core)
        return remote(ref, ref, ps.at[1, j, u, 0], pr.at[1, j, u], sector=partner)

    def panel_pair(j, u, side, which, own):
        k = 2 if own else 3
        ref = panel_at(j, u, side, which)
        return remote(ref, ref, ps.at[k, j, u, 0], pr.at[k, j, u], band=sibling)

    def when_own(f):
        if both:
            f()
        else:
            pl.when(x == 0)(f)

    def when_other(f):
        if both:
            f()
        else:
            pl.when(x == 1)(f)

    def panel_one(j):
        def go():
            @pl.when(b == owner)
            def _():
                for u in range(cuts):
                    for d in range(1, nb):
                        panel_out(j, u, d).start()
                lane = pl.multiple_of((j + x * pieces) * LANES, LANES)

                @pl.loop(0, part)
                def _(p):
                    PB[core * part + p, :, pl.ds(lane, LANES)] = (
                        F[1 + core * part + p, nz:nz + plane, j * LANES:(j + 1) * LANES])
        when_own(go)

    def panel_two(j):
        def go():
            for u in range(cuts):
                @pl.when(b != owner)
                def _():
                    ref = panel_at(j, u, x, core)
                    remote(ref, ref, ps.at[0, j, u, 0], pr.at[0, j, u], band=sibling).wait_recv()
                panel_cross(j, u, x).start()
                panel_pair(j, u, x, core, True).start()
        when_own(go)

    def panel_three(j):
        def go():
            for u in range(cuts):
                panel_cross(j, u, 1 - x).wait_recv()
                panel_pair(j, u, 1 - x, core, False).start()
        when_other(go)

    def panel_ready():
        for j in range(pieces):
            for u in range(cuts):
                when_own(lambda: panel_pair(j, u, x, 1 - core, True).wait_recv())
                when_other(lambda: panel_pair(j, u, 1 - x, 1 - core, False).wait_recv())

        @pl.loop(0, n)
        def _(p):
            PT[p] = PB[p].T

    def panel_done():
        for j in range(pieces):
            for u in range(cuts):
                def own():
                    @pl.when(b == owner)
                    def _():
                        for d in range(1, nb):
                            panel_out(j, u, d).wait_send()
                    panel_cross(j, u, x).wait_send()
                    panel_pair(j, u, x, core, True).wait_send()
                when_own(own)
                when_other(lambda: panel_pair(j, u, 1 - x, core, False).wait_send())

    scale = 1.0 / (plane * n)

    def result_copy(g, k):
        lo, width = batches[g]
        theirs = pl.ds(pl.multiple_of((1 - x) * rows, 8), rows)
        lanes = pl.ds(lo, width)
        src, dst = (PG, RG) if k == 0 else (PH, RH)
        return remote(src.at[theirs, lanes], dst.at[:, lanes], os.at[k, g], orr.at[k, g], sector=partner)

    def write(out, ref, at, g, side):
        lo, width = batches[g]
        for q in range(lo // LANES, (lo + width) // LANES):
            out[:, pl.ds(source_lane(q, side), LANES)] = ref[at, q * LANES:(q + 1) * LANES] * scale

    def project(g, k):
        lo, width = batches[g]
        cs = slice(lo, lo + width)
        total = PG if k == 0 else PH

        def field(p):
            return F[p + 1, nz:nz + plane, cs] if k == 0 else I[p, :, cs]

        def multiply(side):
            at = pl.ds(pl.multiple_of(side * rows, 8), rows)
            value = jnp.dot(PT[0, at, :], field(0), preferred_element_type=F32)
            for p in range(1, n):
                value = value + jnp.dot(PT[p, at, :], field(p), preferred_element_type=F32)
            total[at, cs] = value
            return at

        multiply(1 - x)
        result_copy(g, k).start()
        write(gram if k == 0 else ham, total, multiply(x), g, x)

    def collect(g, k):
        result_copy(g, k).wait_recv()
        write(gram if k == 0 else ham, RG if k == 0 else RH, slice(0, rows), g, 1 - x)

    last_piece = (pieces * LANES - 1) // chunk
    projected = 0
    gather(chunks)
    pump(0, 1)
    pump(0, 2)
    if chunks > 1:
        send_late(1, jnp.logical_not(outermost))
    loads[7].wait()
    loads[8].wait()
    setup()
    for c in range(chunks):
        gather(c)
        if c + 1 < chunks:
            pump(c + 1, 1)
        stage_first(c)
        stage_filtered(c)
        if c < pieces:
            panel_one(c)
        if c == 0:
            if chunks > 1:
                pump(1, 2)
            for later in range(2, chunks):
                send_late(later, jnp.logical_not(outermost))
        if c == chunks - 1:
            if last_piece == c:
                if c > 0:
                    panel_three(c - 1)
                panel_two(c)
                panel_three(c)
                panel_ready()
            last = len(batches) - 1
            if projected == last:
                project(last, 0)
        stage_image(c)
        if c < pieces and c < chunks - 1:
            if c > 0:
                panel_three(c - 1)
                if c + 1 < chunks:
                    pump(c + 1, 2)
                if c + 2 < chunks:
                    pump(c + 2, 1)
            panel_two(c)
            if c == last_piece:
                if c + 2 < chunks:
                    pump(c + 2, 2)
                panel_three(c)
                panel_ready()
        if last_piece <= c < chunks - 1:
            while projected < len(batches) and batches[projected][0] + batches[projected][1] <= (c + 1) * chunk:
                project(projected, 0)
                project(projected, 1)
                projected += 1
    for g in range(projected, len(batches)):
        if g < len(batches) - 1:
            project(g, 0)
        project(g, 1)
    for g in range(len(batches)):
        collect(g, 0)
        collect(g, 1)

    def sent(copy):
        copy.wait_send()

    for c in range(chunks + 1):
        cross(c).wait_send()
        send_plane(c, 0, sent)
        send_plane(c, 1, sent)
        for d in range(1, levels - 1):
            for way in range(2):
                @pl.when(has_source(way, d) & has_target(way))
                def _():
                    sent(relay(c, way, d))
    panel_done()
    for g in range(len(batches)):
        result_copy(g, 0).wait_send()
        result_copy(g, 1).wait_send()


def coefficients(nr, nz):
    plane = nr * nz
    window = BLOCK + 2 * nz
    out = np.zeros((plane, 2 * LANES), np.float64)
    for i in range(nr):
        radius = float(nr + i)
        for z in range(nz):
            row = i * nz + z
            first = row // BLOCK * BLOCK - nz
            terms = {}

            def add(ii, zz, value):
                if 0 <= ii < nr:
                    terms[ii * nz + zz] = terms.get(ii * nz + zz, 0.0) + value

            add(i, z, 2.0 + (nr / radius) ** 2 - CENTER)
            add(i, (z + 1) % nz, -0.5)
            add(i, (z - 1) % nz, -0.5)
            add(i + 1, z, -0.5 * (1.0 + 1.0 / (2.0 * radius)))
            add(i - 1, z, -0.5 * (1.0 - 1.0 / (2.0 * radius)))
            for col, value in terms.items():
                out[row, col - first] = value / HALF_SPAN
                out[row, col - first + window] = value / HALF_SPAN
    return out.astype(np.float32)


def shift_matrices(size, nz):
    row = np.arange(size)[:, None]
    col = np.arange(size)[None, :]
    same = row // nz == col // nz
    gap = (col - row) % nz
    return np.stack([same & (gap == nz - TWIST), same & (gap == TWIST)]).astype(np.float32)


def on_device(n, nb, orbitals, potential, near_points, near_values, far_points, far_values, atom_energy):
    _, nr, nz, cols = orbitals.shape
    plane = nr * nz
    atoms = near_points.shape[0]
    mine = cols // 2
    chunk = LANES
    chunks = mine // chunk
    if chunks >= 4:
        batches = [(0, 2 * chunk)] + [(c * chunk, chunk) for c in range(2, chunks)]
    else:
        batches = [(0, mine)]
    rows = PANEL // n
    panel_dev = PANEL // nb
    pieces = max(panel_dev // LANES // 2, 1)
    hops = n // 2 - 1
    tall = plane + 2 * nz
    vmem = pl.BlockSpec(memory_space=pltpu.VMEM)
    dma = pltpu.SemaphoreType.DMA
    given = (orbitals.reshape(plane, cols), near_points, near_values, far_points, far_values,
             atom_energy.reshape(1, atoms), potential.reshape(nr, nz).T,
             jnp.asarray(coefficients(nr, nz)), jnp.asarray(shift_matrices(plane // 2, nz)).astype(BF16))
    return pl.pallas_call(
        functools.partial(kernel, n, nb, nr, nz, chunk, batches),
        out_shape=(jax.ShapeDtypeStruct((rows, cols), F32),) * 2,
        in_specs=[pl.BlockSpec(memory_space=pltpu.HBM)] * len(given),
        out_specs=(vmem,) * 2,
        scratch_shapes=[pltpu.VMEM(array.shape, array.dtype) for array in given] + [
            pltpu.VMEM((n + 2, tall, mine), BF16),
            pltpu.VMEM((n + 2, tall, chunk), BF16),
            pltpu.VMEM((n + 2, tall, mine), BF16),
            pltpu.VMEM((n, plane, mine), BF16),
            pltpu.VMEM((n, 2 * atoms, LANES), F32),
            pltpu.VMEM((n, 2 * atoms, plane), BF16),
            pltpu.VMEM((n, plane, 2 * LANES), BF16),
            pltpu.VMEM((n, atoms, LANES), F32),
            pltpu.VMEM((n, 2 * atoms, chunk), F32),
            pltpu.VMEM((n, 4 * atoms, chunk), BF16),
            pltpu.VMEM((n, plane, panel_dev), BF16),
            pltpu.VMEM((n, panel_dev, plane), BF16),
            pltpu.VMEM((panel_dev, mine), F32),
            pltpu.VMEM((panel_dev, mine), F32),
            pltpu.VMEM((rows, mine), F32),
            pltpu.VMEM((rows, mine), F32),
            dma((chunks + 1,)),
            dma((chunks + 1,)),
            dma((2, chunks + 1, hops, 2)),
            dma((2, chunks + 1, hops, 2)),
            dma((4, pieces, CUTS, nb)),
            dma((4, pieces, CUTS)),
            dma((2, len(batches))),
            dma((2, len(batches))),
            dma((len(given),)),
        ],
        compiler_params=pltpu.CompilerParams(
            collective_id=0, has_side_effects=True, vmem_limit_bytes=56 * 2 ** 20
        ),
    )(*given)


def solution(mesh):
    n, nb = mesh.shape["sector"], mesh.shape["band"]
    return jax.shard_map(
        functools.partial(on_device, n, nb),
        mesh=mesh,
        in_specs=(
            P("sector", None, None, "band"),
            P("sector", None, None),
            P("sector", None),
            P("sector", None),
            P("sector", None),
            P("sector", None),
            P("sector"),
        ),
        out_specs=(P("sector", "band"), P("sector", "band")),
        check_vma=False,
    )
```

```python
import functools

import jax
import jax.numpy as jnp
import numpy as np
from jax import lax
from jax.experimental import pallas as pl
from jax.experimental.pallas import tpu as pltpu
from jax.sharding import PartitionSpec as P

MESH = pl.DeviceIdType.MESH
F32 = jnp.float32
BF16 = jnp.bfloat16

TWIST = 3
PANEL = 2048
CENTER = 6.0
HALF_SPAN = 3.0
LANES = 128
BLOCK = 64
CUTS = 4


def widen(tile, width):
    return jnp.concatenate([tile] * (width // LANES), axis=1) if width > LANES else tile


def kernel(n, nb, nr, nz, chunk, batches, *refs):
    count = 9
    given, (ham, gram), held = refs[:count], refs[count:count + 2], refs[count + 2:2 * count + 2]
    orb, npts, nval, fpts, fval, energy, pot, base, shifts = held
    (O, A, F, I, BB, W, B, EB, CO, SP, PB, PT, PH, PG, RH, RG,
     xs, xr, zs, zr, ps, pr, os, orr, load) = refs[2 * count + 2:]
    loads = [pltpu.make_async_copy(src, dst, load.at[i]) for i, (src, dst) in enumerate(zip(given, held))]
    for copy in loads[1:7] + loads[:1] + loads[7:]:
        copy.start()
    plane, cols = orb.shape
    rows = ham.shape[0]
    atoms, near_sup = npts.shape
    far_sup = fpts.shape[1]
    half = plane // 2
    mine = cols // 2
    chunks = mine // chunk
    levels = n // 2
    panel_dev = PANEL // nb
    panel_blocks = panel_dev // LANES
    pieces = max(panel_blocks // 2, 1)
    both = panel_blocks >= 2
    order = list(range(pieces)) + ([panel_blocks + j for j in range(pieces)] if both else [])
    window = BLOCK + 2 * nz
    per_block = BLOCK // nz
    s = lax.axis_index("sector")
    b = lax.axis_index("band")
    x = lax.rem(s, 2)
    level = s // 2
    partner = s + 1 - 2 * x
    core = lax.rem(b, 2)
    sibling = b + 1 - 2 * core
    owner = level

    def source_lane(j, side):
        return pl.multiple_of((order[j] + side * pieces) * LANES, LANES)

    def remote(src, dst, send, recv, **device):
        return pltpu.make_async_remote_copy(
            src_ref=src, dst_ref=dst, send_sem=send, recv_sem=recv, device_id=device, device_id_type=MESH)

    def target(way):
        return s + 2 if way == 0 else s - 2

    def has_target(way):
        return level + 1 < levels if way == 0 else level >= 1

    def has_source(way, d):
        return level - d >= 0 if way == 0 else level + d < levels

    def source_level(way, d):
        return level - d if way == 0 else level + d

    barrier = pltpu.get_barrier_semaphore()
    pl.semaphore_signal(barrier, inc=1, device_id={"sector": partner}, device_id_type=MESH)
    for way in range(2):
        @pl.when(has_target(way))
        def _():
            pl.semaphore_signal(barrier, inc=1, device_id={"sector": target(way)}, device_id_type=MESH)
    for d in range(1, nb):
        pl.semaphore_signal(barrier, inc=1, device_id={"band": lax.rem(b + d, nb)}, device_id_type=MESH)

    for copy in loads[1:7]:
        copy.wait()
    eye = lax.broadcasted_iota(jnp.int32, (atoms, atoms), 0) == lax.broadcasted_iota(jnp.int32, (atoms, atoms), 1)
    column = jnp.sum(jnp.where(eye, jnp.broadcast_to(energy[...], (atoms, atoms)), 0.0), axis=1, keepdims=True)
    BB[s, 0:atoms, :] = jnp.concatenate(
        [npts[...].astype(F32), nval[...].astype(F32), fpts[...].astype(F32), fval[...].astype(F32)], axis=1)
    BB[s, atoms:2 * atoms, :] = jnp.concatenate(
        [pot[...], jnp.broadcast_to(column, (atoms, LANES - nr))], axis=1)
    ends = jnp.where(level == 0, 1, 0) + jnp.where(level == levels - 1, 1, 0)
    pl.semaphore_wait(barrier, nb + 2 - ends)

    loads[0].wait()
    per = chunk // LANES

    def place(c, p, count):
        if c == chunks:
            return BB.at[p] if count == 1 else BB.at[pl.ds(p, count)]
        rows_at, lanes_at = pl.ds(nz, plane), pl.ds(c * chunk, chunk)
        return O.at[p + 1, rows_at, lanes_at] if count == 1 else O.at[pl.ds(p + 1, count), rows_at, lanes_at]

    def own_source(c, side):
        return BB.at[s] if c == chunks else orb.at[:, pl.ds(source_lane(c * per, side), chunk)]

    def cross(c):
        return remote(own_source(c, 1 - x), place(c, s, 1), xs.at[c], xr.at[c], sector=partner)

    def cross_wait(c):
        remote(place(c, partner, 1), place(c, partner, 1), xs.at[c], xr.at[c], sector=partner).wait_recv()

    def direct(c, j, way):
        dst = place(c, s if j == 0 else partner, 1)
        return remote(own_source(c, x) if j == 0 else dst, dst,
                      zs.at[way, c, 0, j], zr.at[way, c, 0, j], sector=target(way))

    def relay(c, way, d):
        ref = place(c, 2 * source_level(way, d), 2)
        return remote(ref, ref, zs.at[way, c, d, 0], zr.at[way, c, d, 0], sector=target(way))

    def arrived(c, way, d):
        lv = source_level(way, d)
        if d == 1:
            for j in range(2):
                ref = place(c, 2 * lv + (x if j == 0 else 1 - x), 1)
                remote(ref, ref, zs.at[way, c, 0, j], zr.at[way, c, 0, j], sector=partner).wait_recv()
        else:
            ref = place(c, 2 * lv, 2)
            remote(ref, ref, zs.at[way, c, d - 1, 0], zr.at[way, c, d - 1, 0], sector=partner).wait_recv()

    def send_plane(c, j, act):
        for way in range(2):
            @pl.when(has_target(way))
            def _():
                act(direct(c, j, way))

    pumped = set()

    def pump(c, d):
        if c > chunks or d >= levels - 1 or (c, d) in pumped:
            return
        pumped.add((c, d))
        for way in range(2):
            @pl.when(has_source(way, d) & has_target(way))
            def _():
                arrived(c, way, d)
                relay(c, way, d).start()

    def gather(c):
        for d in range(1, levels):
            pump(c, d)
        for d in range(1, levels):
            for way in range(2):
                here = has_source(way, d)
                if d < levels - 1:
                    here = here & jnp.logical_not(has_target(way))

                @pl.when(here)
                def _():
                    arrived(c, way, d)

    def start(copy):
        copy.start()

    outermost = (level == 0) | (level == levels - 1)

    def send_own(c):
        send_plane(c, 0, start)
        cross_wait(c)
        send_plane(c, 1, start)

    def send_late(c, when):
        @pl.when(when)
        def _():
            send_own(c)

    cross(chunks).start()
    for c in range(chunks):
        cross(c).start()
    send_plane(chunks, 0, start)
    send_plane(0, 0, start)
    for j in range(mine // LANES):
        O[s + 1, nz:nz + plane, j * LANES:(j + 1) * LANES] = orb[:, pl.ds(source_lane(j, x), LANES)]
    cross_wait(chunks)
    send_plane(chunks, 1, start)
    cross_wait(0)
    send_plane(0, 1, start)
    for c in range(1, chunks):
        send_late(c, outermost)

    for ref, width in ((O, mine), (F, mine), (A, chunk)):
        @pl.loop(0, n)
        def _(p):
            ref[p + 1, 0:nz, :] = jnp.zeros((nz, width), BF16)
            ref[p + 1, nz + plane:nz + plane + nz, :] = jnp.zeros((nz, width), BF16)

    def setup():
        lane = lax.broadcasted_iota(jnp.int32, (BLOCK, 2 * LANES), 1)
        row = lax.broadcasted_iota(jnp.int32, (BLOCK, 2 * LANES), 0)
        diagonal = (lane == row + nz) | (lane == row + nz + window)
        ids = lax.broadcasted_iota(jnp.int32, (atoms, plane), 1).astype(F32)

        @pl.loop(0, n)
        def _(p):
            packed = BB[p, 0:atoms, :]

            def dense(at, count):
                total = jnp.zeros((atoms, plane), F32)
                for j in range(count):
                    point = packed[:, at + j:at + j + 1]
                    value = packed[:, at + count + j:at + count + j + 1]
                    total = total + jnp.where(ids == point, value, 0.0)
                return total.astype(BF16).astype(F32)

            near = dense(0, near_sup)
            far = dense(2 * near_sup, far_sup)
            both_parts = jnp.concatenate([near, far], axis=0)
            W[p] = both_parts.astype(BF16)
            turned = jnp.concatenate([both_parts] * (LANES // (2 * atoms)), axis=0).T
            local = BB[p, atoms:2 * atoms, :]
            EB[p] = jnp.broadcast_to(local[:, nr:nr + 1] * (1.0 / HALF_SPAN), (atoms, LANES))
            for q in range(plane // BLOCK):
                at = slice(q * BLOCK, (q + 1) * BLOCK)
                level_pot = jnp.concatenate(
                    [jnp.broadcast_to(local[:, i:i + 1], (nz, 2 * LANES))
                     for i in range(q * per_block, (q + 1) * per_block)], axis=0)
                value = base[at, :] + jnp.where(diagonal, level_pot * (1.0 / HALF_SPAN), 0.0)
                high = value.astype(BF16).astype(F32)
                tail = jnp.concatenate([turned[at, :]] * 2, axis=1)
                B[p, at, :] = jnp.where(
                    lane < window, high, jnp.where(lane < 2 * window, value - high, tail)).astype(BF16)

    def prepare(v, cs):
        for h in range(2):
            r = nz + h * half
            v[0, r:r + half, cs] = jnp.dot(shifts[0], v[n, r:r + half, cs], preferred_element_type=F32).astype(BF16)
            v[n + 1, r:r + half, cs] = jnp.dot(shifts[1], v[1, r:r + half, cs], preferred_element_type=F32).astype(BF16)

        @pl.loop(0, n, unroll=8)
        def _(p):
            CO[p] = jnp.dot(W[p], v[p + 1, nz:nz + plane, cs], preferred_element_type=F32)

        @pl.loop(0, n, unroll=8)
        def _(p):
            after = lax.rem(p + 1, n)
            rest = widen(EB[p], chunk) * (CO[p, 0:atoms, :] + CO[after, atoms:2 * atoms, :])
            for term in range(2):
                part = rest.astype(BF16)
                rest = rest - part.astype(F32)
                r = term * 2 * atoms
                SP[p, r:r + atoms, :] = part
                SP[after, r + atoms:r + 2 * atoms, :] = part

    def operate(v, cs, finish):
        prepare(v, cs)

        @pl.loop(0, n, unroll=4)
        def _(p):
            terms = SP[p]
            for q in range(plane // BLOCK):
                r = nz + q * BLOCK
                near_rows = v[p + 1, r - nz:r + BLOCK + nz, cs]
                total = jnp.dot(B[p, q * BLOCK:(q + 1) * BLOCK, :],
                                jnp.concatenate([near_rows, near_rows, terms], axis=0),
                                preferred_element_type=F32)
                for k in range(per_block):
                    i = q * per_block + k
                    at = r + k * nz
                    sides = v[p + 2, at:at + nz, cs].astype(F32) + v[p, at:at + nz, cs].astype(F32)
                    weight = -0.5 * (nr / (nr + i)) ** 2 / HALF_SPAN
                    finish(p, at, total[k * nz:(k + 1) * nz] + weight * sides)

    def chunk_lanes(c):
        return slice(c * chunk, (c + 1) * chunk)

    def stage_first(c):
        def finish(p, r, value):
            A[p + 1, r:r + nz, :] = value.astype(BF16)

        operate(O, chunk_lanes(c), finish)

    def stage_filtered(c):
        cs = chunk_lanes(c)

        def finish(p, r, value):
            F[p + 1, r:r + nz, cs] = (2.0 * value - O[p + 1, r:r + nz, cs].astype(F32)).astype(BF16)

        operate(A, slice(0, chunk), finish)

    def stage_image(c):
        cs = chunk_lanes(c)

        def finish(p, r, value):
            I[p, r - nz:r, cs] = (HALF_SPAN * value + CENTER * F[p + 1, r:r + nz, cs].astype(F32)).astype(BF16)

        operate(F, cs, finish)

    part = n // 2
    cuts = CUTS
    run = part // cuts

    def panel_at(j, u, side, which):
        lane = pl.multiple_of((j + side * pieces) * LANES, LANES)
        return PB.at[pl.ds(which * part + u * run, run), :, pl.ds(lane, LANES)]

    def panel_out(j, u, d):
        to = lax.rem(b + d, nb)
        which = lax.rem(to, 2)
        return remote(F.at[pl.ds(1 + which * part + u * run, run), pl.ds(nz, plane), pl.ds(j * LANES, LANES)],
                      panel_at(j, u, x, which), ps.at[0, j, u, d], pr.at[0, j, u], band=to)

    def panel_cross(j, u, side):
        ref = panel_at(j, u, side, core)
        return remote(ref, ref, ps.at[1, j, u, 0], pr.at[1, j, u], sector=partner)

    def panel_pair(j, u, side, which, own):
        k = 2 if own else 3
        ref = panel_at(j, u, side, which)
        return remote(ref, ref, ps.at[k, j, u, 0], pr.at[k, j, u], band=sibling)

    def when_own(f):
        if both:
            f()
        else:
            pl.when(x == 0)(f)

    def when_other(f):
        if both:
            f()
        else:
            pl.when(x == 1)(f)

    def panel_one(j):
        def go():
            @pl.when(b == owner)
            def _():
                for u in range(cuts):
                    for d in range(1, nb):
                        panel_out(j, u, d).start()
                lane = pl.multiple_of((j + x * pieces) * LANES, LANES)

                @pl.loop(0, part)
                def _(p):
                    PB[core * part + p, :, pl.ds(lane, LANES)] = (
                        F[1 + core * part + p, nz:nz + plane, j * LANES:(j + 1) * LANES])
        when_own(go)

    def panel_two(j):
        def go():
            for u in range(cuts):
                @pl.when(b != owner)
                def _():
                    ref = panel_at(j, u, x, core)
                    remote(ref, ref, ps.at[0, j, u, 0], pr.at[0, j, u], band=sibling).wait_recv()
                panel_cross(j, u, x).start()
                panel_pair(j, u, x, core, True).start()
        when_own(go)

    def panel_three(j):
        def go():
            for u in range(cuts):
                panel_cross(j, u, 1 - x).wait_recv()
                panel_pair(j, u, 1 - x, core, False).start()
        when_other(go)

    groups = pieces if both else 1
    group_rows = rows // groups

    def panel_ready(j):
        for u in range(cuts):
            when_own(lambda: panel_pair(j, u, x, 1 - core, True).wait_recv())
            when_other(lambda: panel_pair(j, u, 1 - x, 1 - core, False).wait_recv())

        @pl.loop(0, n)
        def _(p):
            for block in (j, j + pieces) if both else (j,):
                lanes = slice(block * LANES, (block + 1) * LANES)
                PT[p, lanes, :] = PB[p, :, lanes].T

    def panel_done():
        for j in range(pieces):
            for u in range(cuts):
                def own():
                    @pl.when(b == owner)
                    def _():
                        for d in range(1, nb):
                            panel_out(j, u, d).wait_send()
                    panel_cross(j, u, x).wait_send()
                    panel_pair(j, u, x, core, True).wait_send()
                when_own(own)
                when_other(lambda: panel_pair(j, u, 1 - x, core, False).wait_send())

    scale = 1.0 / (plane * n)

    def result_copy(g, k, j):
        lo, width = batches[g]
        theirs = pl.ds(pl.multiple_of((1 - x) * rows + j * group_rows, 8), group_rows)
        lanes = pl.ds(lo, width)
        src, dst = (PG, RG) if k == 0 else (PH, RH)
        return remote(src.at[theirs, lanes], dst.at[pl.ds(j * group_rows, group_rows), lanes],
                      os.at[k, g, j], orr.at[k, g, j], sector=partner)

    def write(out, ref, at, g, side):
        lo, width = batches[g]
        for q in range(lo // LANES, (lo + width) // LANES):
            out[:, pl.ds(source_lane(q, side), LANES)] = ref[at, q * LANES:(q + 1) * LANES] * scale

    def multiply(g, k, offset, count):
        lo, width = batches[g]
        cs = slice(lo, lo + width)
        total = PG if k == 0 else PH
        at = pl.ds(pl.multiple_of(offset, 8), count)

        def field(p):
            return F[p + 1, nz:nz + plane, cs] if k == 0 else I[p, :, cs]

        value = jnp.dot(PT[0, at, :], field(0), preferred_element_type=F32)
        for p in range(1, n):
            value = value + jnp.dot(PT[p, at, :], field(p), preferred_element_type=F32)
        total[at, cs] = value

    def project_theirs(g, k, j):
        multiply(g, k, (1 - x) * rows + j * group_rows, group_rows)
        result_copy(g, k, j).start()

    def project_ours(g, k):
        multiply(g, k, x * rows, rows)
        write(gram if k == 0 else ham, PG if k == 0 else PH, pl.ds(pl.multiple_of(x * rows, 8), rows), g, x)

    def project(g, k):
        multiply(g, k, (1 - x) * rows, rows)
        for j in range(groups):
            result_copy(g, k, j).start()
        project_ours(g, k)

    def collect(g, k):
        for j in range(groups):
            result_copy(g, k, j).wait_recv()
        write(gram if k == 0 else ham, RG if k == 0 else RH, slice(0, rows), g, 1 - x)

    last_piece = (pieces * LANES - 1) // chunk
    projected = 0
    gather(chunks)
    pump(0, 1)
    pump(0, 2)
    if chunks > 1:
        send_late(1, jnp.logical_not(outermost))
    loads[7].wait()
    loads[8].wait()
    setup()
    for c in range(chunks):
        gather(c)
        if c + 1 < chunks:
            pump(c + 1, 1)
        stage_first(c)
        stage_filtered(c)
        if c < pieces:
            panel_one(c)
        if c == 0:
            if chunks > 1:
                pump(1, 2)
            for later in range(2, chunks):
                send_late(later, jnp.logical_not(outermost))
        if c == chunks - 1:
            if last_piece == c:
                if c > 0:
                    panel_three(c - 1)
                panel_two(c)
                panel_three(c)
                for j in range(pieces):
                    panel_ready(j)
            last = len(batches) - 1
            if projected == last:
                project(last, 0)
        stage_image(c)
        if c < pieces and c < chunks - 1:
            if c > 0:
                panel_three(c - 1)
                if c + 1 < chunks:
                    pump(c + 1, 2)
                if c + 2 < chunks:
                    pump(c + 2, 1)
            panel_two(c)
            if c == last_piece:
                if c + 2 < chunks:
                    pump(c + 2, 2)
                early = groups > 1 and batches[0][0] + batches[0][1] == (c + 1) * chunk
                for j in range(pieces - 1):
                    panel_ready(j)
                    if early:
                        project_theirs(0, 0, j)
                        project_theirs(0, 1, j)
                panel_three(c)
                panel_ready(c)
                if early:
                    project_theirs(0, 0, c)
                    project_theirs(0, 1, c)
                    project_ours(0, 0)
                    project_ours(0, 1)
                    projected = 1
        if last_piece <= c < chunks - 1:
            while projected < len(batches) and batches[projected][0] + batches[projected][1] <= (c + 1) * chunk:
                project(projected, 0)
                project(projected, 1)
                projected += 1
    for g in range(projected, len(batches)):
        if g < len(batches) - 1:
            project(g, 0)
        project(g, 1)
    for g in range(len(batches)):
        collect(g, 0)
        collect(g, 1)

    def sent(copy):
        copy.wait_send()

    for c in range(chunks + 1):
        cross(c).wait_send()
        send_plane(c, 0, sent)
        send_plane(c, 1, sent)
        for d in range(1, levels - 1):
            for way in range(2):
                @pl.when(has_source(way, d) & has_target(way))
                def _():
                    sent(relay(c, way, d))
    panel_done()
    for g in range(len(batches)):
        for j in range(groups):
            result_copy(g, 0, j).wait_send()
            result_copy(g, 1, j).wait_send()


def coefficients(nr, nz):
    plane = nr * nz
    window = BLOCK + 2 * nz
    out = np.zeros((plane, 2 * LANES), np.float64)
    for i in range(nr):
        radius = float(nr + i)
        for z in range(nz):
            row = i * nz + z
            first = row // BLOCK * BLOCK - nz
            terms = {}

            def add(ii, zz, value):
                if 0 <= ii < nr:
                    terms[ii * nz + zz] = terms.get(ii * nz + zz, 0.0) + value

            add(i, z, 2.0 + (nr / radius) ** 2 - CENTER)
            add(i, (z + 1) % nz, -0.5)
            add(i, (z - 1) % nz, -0.5)
            add(i + 1, z, -0.5 * (1.0 + 1.0 / (2.0 * radius)))
            add(i - 1, z, -0.5 * (1.0 - 1.0 / (2.0 * radius)))
            for col, value in terms.items():
                out[row, col - first] = value / HALF_SPAN
                out[row, col - first + window] = value / HALF_SPAN
    return out.astype(np.float32)


def shift_matrices(size, nz):
    row = np.arange(size)[:, None]
    col = np.arange(size)[None, :]
    same = row // nz == col // nz
    gap = (col - row) % nz
    return np.stack([same & (gap == nz - TWIST), same & (gap == TWIST)]).astype(np.float32)


def on_device(n, nb, orbitals, potential, near_points, near_values, far_points, far_values, atom_energy):
    _, nr, nz, cols = orbitals.shape
    plane = nr * nz
    atoms = near_points.shape[0]
    mine = cols // 2
    chunk = LANES
    chunks = mine // chunk
    if chunks >= 4:
        batches = [(0, 2 * chunk)] + [(c * chunk, chunk) for c in range(2, chunks)]
    else:
        batches = [(0, mine)]
    rows = PANEL // n
    panel_dev = PANEL // nb
    pieces = max(panel_dev // LANES // 2, 1)
    hops = n // 2 - 1
    tall = plane + 2 * nz
    vmem = pl.BlockSpec(memory_space=pltpu.VMEM)
    dma = pltpu.SemaphoreType.DMA
    given = (orbitals.reshape(plane, cols), near_points, near_values, far_points, far_values,
             atom_energy.reshape(1, atoms), potential.reshape(nr, nz).T,
             jnp.asarray(coefficients(nr, nz)), jnp.asarray(shift_matrices(plane // 2, nz)).astype(BF16))
    return pl.pallas_call(
        functools.partial(kernel, n, nb, nr, nz, chunk, batches),
        out_shape=(jax.ShapeDtypeStruct((rows, cols), F32),) * 2,
        in_specs=[pl.BlockSpec(memory_space=pltpu.HBM)] * len(given),
        out_specs=(vmem,) * 2,
        scratch_shapes=[pltpu.VMEM(array.shape, array.dtype) for array in given] + [
            pltpu.VMEM((n + 2, tall, mine), BF16),
            pltpu.VMEM((n + 2, tall, chunk), BF16),
            pltpu.VMEM((n + 2, tall, mine), BF16),
            pltpu.VMEM((n, plane, mine), BF16),
            pltpu.VMEM((n, 2 * atoms, LANES), F32),
            pltpu.VMEM((n, 2 * atoms, plane), BF16),
            pltpu.VMEM((n, plane, 2 * LANES), BF16),
            pltpu.VMEM((n, atoms, LANES), F32),
            pltpu.VMEM((n, 2 * atoms, chunk), F32),
            pltpu.VMEM((n, 4 * atoms, chunk), BF16),
            pltpu.VMEM((n, plane, panel_dev), BF16),
            pltpu.VMEM((n, panel_dev, plane), BF16),
            pltpu.VMEM((panel_dev, mine), F32),
            pltpu.VMEM((panel_dev, mine), F32),
            pltpu.VMEM((rows, mine), F32),
            pltpu.VMEM((rows, mine), F32),
            dma((chunks + 1,)),
            dma((chunks + 1,)),
            dma((2, chunks + 1, hops, 2)),
            dma((2, chunks + 1, hops, 2)),
            dma((4, pieces, CUTS, nb)),
            dma((4, pieces, CUTS)),
            dma((2, len(batches), pieces)),
            dma((2, len(batches), pieces)),
            dma((len(given),)),
        ],
        compiler_params=pltpu.CompilerParams(
            collective_id=0, has_side_effects=True, vmem_limit_bytes=56 * 2 ** 20
        ),
    )(*given)


def solution(mesh):
    n, nb = mesh.shape["sector"], mesh.shape["band"]
    return jax.shard_map(
        functools.partial(on_device, n, nb),
        mesh=mesh,
        in_specs=(
            P("sector", None, None, "band"),
            P("sector", None, None),
            P("sector", None),
            P("sector", None),
            P("sector", None),
            P("sector", None),
            P("sector"),
        ),
        out_specs=(P("sector", "band"), P("sector", "band")),
        check_vma=False,
    )
```

```python
import functools

import jax
import jax.numpy as jnp
import numpy as np
from jax import lax
from jax.experimental import pallas as pl
from jax.experimental.pallas import tpu as pltpu
from jax.sharding import PartitionSpec as P

MESH = pl.DeviceIdType.MESH
F32 = jnp.float32
BF16 = jnp.bfloat16

TWIST = 3
PANEL = 2048
CENTER = 6.0
HALF_SPAN = 3.0
LANES = 128
BLOCK = 64
CUTS = 4


def widen(tile, width):
    return jnp.concatenate([tile] * (width // LANES), axis=1) if width > LANES else tile


def kernel(n, nb, nr, nz, chunk, batches, *refs):
    count = 9
    given, (ham, gram), held = refs[:count], refs[count:count + 2], refs[count + 2:2 * count + 2]
    orb, npts, nval, fpts, fval, energy, pot, base, shifts = held
    (O, A, F, I, BB, W, B, EB, CO, SP, PB, PT, PH, PG, RH, RG,
     xs, xr, zs, zr, ps, pr, os, orr, load) = refs[2 * count + 2:]
    loads = [pltpu.make_async_copy(src, dst, load.at[i]) for i, (src, dst) in enumerate(zip(given, held))]
    for copy in loads[1:7] + loads[:1] + loads[7:]:
        copy.start()
    plane, cols = orb.shape
    rows = ham.shape[0]
    atoms, near_sup = npts.shape
    far_sup = fpts.shape[1]
    half = plane // 2
    mine = cols // 2
    chunks = mine // chunk
    levels = n // 2
    panel_dev = PANEL // nb
    panel_blocks = panel_dev // LANES
    pieces = max(panel_blocks // 2, 1)
    both = panel_blocks >= 2
    order = list(range(pieces)) + ([panel_blocks + j for j in range(pieces)] if both else [])
    window = BLOCK + 2 * nz
    per_block = BLOCK // nz
    s = lax.axis_index("sector")
    b = lax.axis_index("band")
    x = lax.rem(s, 2)
    level = s // 2
    partner = s + 1 - 2 * x
    core = lax.rem(b, 2)
    sibling = b + 1 - 2 * core
    owner = level

    def source_lane(j, side):
        return pl.multiple_of((order[j] + side * pieces) * LANES, LANES)

    def remote(src, dst, send, recv, **device):
        return pltpu.make_async_remote_copy(
            src_ref=src, dst_ref=dst, send_sem=send, recv_sem=recv, device_id=device, device_id_type=MESH)

    def target(way):
        return s + 2 if way == 0 else s - 2

    def has_target(way):
        return level + 1 < levels if way == 0 else level >= 1

    def has_source(way, d):
        return level - d >= 0 if way == 0 else level + d < levels

    def source_level(way, d):
        return level - d if way == 0 else level + d

    barrier = pltpu.get_barrier_semaphore()
    pl.semaphore_signal(barrier, inc=1, device_id={"sector": partner}, device_id_type=MESH)
    for way in range(2):
        @pl.when(has_target(way))
        def _():
            pl.semaphore_signal(barrier, inc=1, device_id={"sector": target(way)}, device_id_type=MESH)
    for d in range(1, nb):
        pl.semaphore_signal(barrier, inc=1, device_id={"band": lax.rem(b + d, nb)}, device_id_type=MESH)

    for copy in loads[1:7]:
        copy.wait()
    eye = lax.broadcasted_iota(jnp.int32, (atoms, atoms), 0) == lax.broadcasted_iota(jnp.int32, (atoms, atoms), 1)
    column = jnp.sum(jnp.where(eye, jnp.broadcast_to(energy[...], (atoms, atoms)), 0.0), axis=1, keepdims=True)
    BB[s, 0:atoms, :] = jnp.concatenate(
        [npts[...].astype(F32), nval[...].astype(F32), fpts[...].astype(F32), fval[...].astype(F32)], axis=1)
    BB[s, atoms:2 * atoms, :] = jnp.concatenate(
        [pot[...], jnp.broadcast_to(column, (atoms, LANES - nr))], axis=1)
    ends = jnp.where(level == 0, 1, 0) + jnp.where(level == levels - 1, 1, 0)
    pl.semaphore_wait(barrier, nb + 2 - ends)

    loads[0].wait()
    per = chunk // LANES

    def place(c, p, count):
        if c == chunks:
            return BB.at[p] if count == 1 else BB.at[pl.ds(p, count)]
        rows_at, lanes_at = pl.ds(nz, plane), pl.ds(c * chunk, chunk)
        return O.at[p + 1, rows_at, lanes_at] if count == 1 else O.at[pl.ds(p + 1, count), rows_at, lanes_at]

    def own_source(c, side):
        return BB.at[s] if c == chunks else orb.at[:, pl.ds(source_lane(c * per, side), chunk)]

    def cross(c):
        return remote(own_source(c, 1 - x), place(c, s, 1), xs.at[c], xr.at[c], sector=partner)

    def cross_wait(c):
        remote(place(c, partner, 1), place(c, partner, 1), xs.at[c], xr.at[c], sector=partner).wait_recv()

    def direct(c, j, way):
        dst = place(c, s if j == 0 else partner, 1)
        return remote(own_source(c, x) if j == 0 else dst, dst,
                      zs.at[way, c, 0, j], zr.at[way, c, 0, j], sector=target(way))

    def relay(c, way, d):
        ref = place(c, 2 * source_level(way, d), 2)
        return remote(ref, ref, zs.at[way, c, d, 0], zr.at[way, c, d, 0], sector=target(way))

    def arrived(c, way, d):
        lv = source_level(way, d)
        if d == 1:
            for j in range(2):
                ref = place(c, 2 * lv + (x if j == 0 else 1 - x), 1)
                remote(ref, ref, zs.at[way, c, 0, j], zr.at[way, c, 0, j], sector=partner).wait_recv()
        else:
            ref = place(c, 2 * lv, 2)
            remote(ref, ref, zs.at[way, c, d - 1, 0], zr.at[way, c, d - 1, 0], sector=partner).wait_recv()

    def send_plane(c, j, act):
        for way in range(2):
            @pl.when(has_target(way))
            def _():
                act(direct(c, j, way))

    pumped = set()

    def pump(c, d):
        if c > chunks or d >= levels - 1 or (c, d) in pumped:
            return
        pumped.add((c, d))
        for way in range(2):
            @pl.when(has_source(way, d) & has_target(way))
            def _():
                arrived(c, way, d)
                relay(c, way, d).start()

    def gather(c):
        for d in range(1, levels):
            pump(c, d)
        for d in range(1, levels):
            for way in range(2):
                here = has_source(way, d)
                if d < levels - 1:
                    here = here & jnp.logical_not(has_target(way))

                @pl.when(here)
                def _():
                    arrived(c, way, d)

    def start(copy):
        copy.start()

    outermost = (level == 0) | (level == levels - 1)

    def send_own(c):
        send_plane(c, 0, start)
        cross_wait(c)
        send_plane(c, 1, start)

    def send_late(c, when):
        @pl.when(when)
        def _():
            send_own(c)

    cross(chunks).start()
    for c in range(chunks):
        cross(c).start()
    send_plane(chunks, 0, start)
    send_plane(0, 0, start)
    for j in range(mine // LANES):
        O[s + 1, nz:nz + plane, j * LANES:(j + 1) * LANES] = orb[:, pl.ds(source_lane(j, x), LANES)]
    cross_wait(chunks)
    send_plane(chunks, 1, start)
    cross_wait(0)
    send_plane(0, 1, start)
    for c in range(1, chunks):
        send_late(c, outermost)

    for ref, width in ((O, mine), (F, mine), (A, chunk)):
        @pl.loop(0, n)
        def _(p):
            ref[p + 1, 0:nz, :] = jnp.zeros((nz, width), BF16)
            ref[p + 1, nz + plane:nz + plane + nz, :] = jnp.zeros((nz, width), BF16)

    def setup():
        lane = lax.broadcasted_iota(jnp.int32, (BLOCK, 2 * LANES), 1)
        row = lax.broadcasted_iota(jnp.int32, (BLOCK, 2 * LANES), 0)
        diagonal = (lane == row + nz) | (lane == row + nz + window)
        ids = lax.broadcasted_iota(jnp.int32, (atoms, plane), 1).astype(F32)

        @pl.loop(0, n)
        def _(p):
            packed = BB[p, 0:atoms, :]

            def dense(at, count):
                total = jnp.zeros((atoms, plane), F32)
                for j in range(count):
                    point = packed[:, at + j:at + j + 1]
                    value = packed[:, at + count + j:at + count + j + 1]
                    total = total + jnp.where(ids == point, value, 0.0)
                return total.astype(BF16).astype(F32)

            near = dense(0, near_sup)
            far = dense(2 * near_sup, far_sup)
            both_parts = jnp.concatenate([near, far], axis=0)
            W[p] = both_parts.astype(BF16)
            turned = jnp.concatenate([both_parts] * (LANES // (2 * atoms)), axis=0).T
            local = BB[p, atoms:2 * atoms, :]
            EB[p] = jnp.broadcast_to(local[:, nr:nr + 1] * (1.0 / HALF_SPAN), (atoms, LANES))
            for q in range(plane // BLOCK):
                at = slice(q * BLOCK, (q + 1) * BLOCK)
                level_pot = jnp.concatenate(
                    [jnp.broadcast_to(local[:, i:i + 1], (nz, 2 * LANES))
                     for i in range(q * per_block, (q + 1) * per_block)], axis=0)
                value = base[at, :] + jnp.where(diagonal, level_pot * (1.0 / HALF_SPAN), 0.0)
                high = value.astype(BF16).astype(F32)
                tail = jnp.concatenate([turned[at, :]] * 2, axis=1)
                B[p, at, :] = jnp.where(
                    lane < window, high, jnp.where(lane < 2 * window, value - high, tail)).astype(BF16)

    def prepare(v, cs):
        for h in range(2):
            r = nz + h * half
            v[0, r:r + half, cs] = jnp.dot(shifts[0], v[n, r:r + half, cs], preferred_element_type=F32).astype(BF16)
            v[n + 1, r:r + half, cs] = jnp.dot(shifts[1], v[1, r:r + half, cs], preferred_element_type=F32).astype(BF16)

        @pl.loop(0, n, unroll=8)
        def _(p):
            CO[p] = jnp.dot(W[p], v[p + 1, nz:nz + plane, cs], preferred_element_type=F32)

        @pl.loop(0, n, unroll=8)
        def _(p):
            after = lax.rem(p + 1, n)
            rest = widen(EB[p], chunk) * (CO[p, 0:atoms, :] + CO[after, atoms:2 * atoms, :])
            for term in range(2):
                part = rest.astype(BF16)
                rest = rest - part.astype(F32)
                r = term * 2 * atoms
                SP[p, r:r + atoms, :] = part
                SP[after, r + atoms:r + 2 * atoms, :] = part

    def operate(v, cs, finish):
        prepare(v, cs)

        @pl.loop(0, n, unroll=4)
        def _(p):
            terms = SP[p]
            for q in range(plane // BLOCK):
                r = nz + q * BLOCK
                near_rows = v[p + 1, r - nz:r + BLOCK + nz, cs]
                total = jnp.dot(B[p, q * BLOCK:(q + 1) * BLOCK, :],
                                jnp.concatenate([near_rows, near_rows, terms], axis=0),
                                preferred_element_type=F32)
                for k in range(per_block):
                    i = q * per_block + k
                    at = r + k * nz
                    sides = v[p + 2, at:at + nz, cs].astype(F32) + v[p, at:at + nz, cs].astype(F32)
                    weight = -0.5 * (nr / (nr + i)) ** 2 / HALF_SPAN
                    finish(p, at, total[k * nz:(k + 1) * nz] + weight * sides)

    def chunk_lanes(c):
        return slice(c * chunk, (c + 1) * chunk)

    def stage_first(c):
        def finish(p, r, value):
            A[p + 1, r:r + nz, :] = value.astype(BF16)

        operate(O, chunk_lanes(c), finish)

    def stage_filtered(c):
        cs = chunk_lanes(c)

        def finish(p, r, value):
            F[p + 1, r:r + nz, cs] = (2.0 * value - O[p + 1, r:r + nz, cs].astype(F32)).astype(BF16)

        operate(A, slice(0, chunk), finish)

    def stage_image(c):
        cs = chunk_lanes(c)

        def finish(p, r, value):
            I[p, r - nz:r, cs] = (HALF_SPAN * value + CENTER * F[p + 1, r:r + nz, cs].astype(F32)).astype(BF16)

        operate(F, cs, finish)

    part = n // 2
    cuts = CUTS
    run = part // cuts

    def panel_at(j, u, side, which):
        lane = pl.multiple_of((j + side * pieces) * LANES, LANES)
        return PB.at[pl.ds(which * part + u * run, run), :, pl.ds(lane, LANES)]

    def panel_out(j, u, d):
        to = lax.rem(b + d, nb)
        which = lax.rem(to, 2)
        return remote(F.at[pl.ds(1 + which * part + u * run, run), pl.ds(nz, plane), pl.ds(j * LANES, LANES)],
                      panel_at(j, u, x, which), ps.at[0, j, u, d], pr.at[0, j, u], band=to)

    def panel_cross(j, u, side):
        ref = panel_at(j, u, side, core)
        return remote(ref, ref, ps.at[1, j, u, 0], pr.at[1, j, u], sector=partner)

    def panel_pair(j, u, side, which, own):
        k = 2 if own else 3
        ref = panel_at(j, u, side, which)
        return remote(ref, ref, ps.at[k, j, u, 0], pr.at[k, j, u], band=sibling)

    def when_own(f):
        if both:
            f()
        else:
            pl.when(x == 0)(f)

    def when_other(f):
        if both:
            f()
        else:
            pl.when(x == 1)(f)

    def panel_one(j):
        def go():
            @pl.when(b == owner)
            def _():
                for u in range(cuts):
                    for d in range(1, nb):
                        panel_out(j, u, d).start()
                lane = pl.multiple_of((j + x * pieces) * LANES, LANES)

                @pl.loop(0, part)
                def _(p):
                    PB[core * part + p, :, pl.ds(lane, LANES)] = (
                        F[1 + core * part + p, nz:nz + plane, j * LANES:(j + 1) * LANES])
        when_own(go)

    def panel_two(j):
        def go():
            for u in range(cuts):
                @pl.when(b != owner)
                def _():
                    ref = panel_at(j, u, x, core)
                    remote(ref, ref, ps.at[0, j, u, 0], pr.at[0, j, u], band=sibling).wait_recv()
                panel_cross(j, u, x).start()
                panel_pair(j, u, x, core, True).start()
        when_own(go)

    def panel_three(j):
        def go():
            for u in range(cuts):
                panel_cross(j, u, 1 - x).wait_recv()
                panel_pair(j, u, 1 - x, core, False).start()
        when_other(go)

    groups = pieces if both else 1
    group_rows = rows // groups

    def panel_ready(j):
        for u in range(cuts):
            when_own(lambda: panel_pair(j, u, x, 1 - core, True).wait_recv())
            when_other(lambda: panel_pair(j, u, 1 - x, 1 - core, False).wait_recv())

        @pl.loop(0, n)
        def _(p):
            for block in (j, j + pieces) if both else (j,):
                lanes = slice(block * LANES, (block + 1) * LANES)
                PT[p, lanes, :] = PB[p, :, lanes].T

    def panel_done():
        for j in range(pieces):
            for u in range(cuts):
                def own():
                    @pl.when(b == owner)
                    def _():
                        for d in range(1, nb):
                            panel_out(j, u, d).wait_send()
                    panel_cross(j, u, x).wait_send()
                    panel_pair(j, u, x, core, True).wait_send()
                when_own(own)
                when_other(lambda: panel_pair(j, u, 1 - x, core, False).wait_send())

    scale = 1.0 / (plane * n)

    def result_copy(g, k, j):
        lo, width = batches[g]
        theirs = pl.ds(pl.multiple_of((1 - x) * rows + j * group_rows, 8), group_rows)
        lanes = pl.ds(lo, width)
        src, dst = (PG, RG) if k == 0 else (PH, RH)
        return remote(src.at[theirs, lanes], dst.at[pl.ds(j * group_rows, group_rows), lanes],
                      os.at[k, g, j], orr.at[k, g, j], sector=partner)

    def write(out, ref, at, g, side):
        lo, width = batches[g]
        for q in range(lo // LANES, (lo + width) // LANES):
            out[:, pl.ds(source_lane(q, side), LANES)] = ref[at, q * LANES:(q + 1) * LANES] * scale

    def multiply(g, k, offset, count):
        lo, width = batches[g]
        cs = slice(lo, lo + width)
        total = PG if k == 0 else PH
        at = pl.ds(pl.multiple_of(offset, 8), count)

        def field(p):
            return F[p + 1, nz:nz + plane, cs] if k == 0 else I[p, :, cs]

        value = jnp.dot(PT[0, at, :], field(0), preferred_element_type=F32)
        for p in range(1, n):
            value = value + jnp.dot(PT[p, at, :], field(p), preferred_element_type=F32)
        total[at, cs] = value

    def project_theirs(g, k, j):
        multiply(g, k, (1 - x) * rows + j * group_rows, group_rows)
        result_copy(g, k, j).start()

    def project_ours(g, k):
        multiply(g, k, x * rows, rows)
        write(gram if k == 0 else ham, PG if k == 0 else PH, pl.ds(pl.multiple_of(x * rows, 8), rows), g, x)

    def project(g, k):
        multiply(g, k, (1 - x) * rows, rows)
        for j in range(groups):
            result_copy(g, k, j).start()
        project_ours(g, k)

    def collect(g, k):
        for j in range(groups):
            result_copy(g, k, j).wait_recv()
        write(gram if k == 0 else ham, RG if k == 0 else RH, slice(0, rows), g, 1 - x)

    last_piece = (pieces * LANES - 1) // chunk
    projected = 0
    gather(chunks)
    pump(0, 1)
    pump(0, 2)
    if chunks > 1:
        send_late(1, jnp.logical_not(outermost))
    loads[7].wait()
    loads[8].wait()
    setup()
    for c in range(chunks):
        gather(c)
        if c + 1 < chunks:
            pump(c + 1, 1)
        stage_first(c)
        stage_filtered(c)
        if c < pieces:
            panel_one(c)
        if c == 0:
            if chunks > 1:
                pump(1, 2)
            for later in range(2, chunks):
                send_late(later, jnp.logical_not(outermost))
        if c == chunks - 1:
            if last_piece == c:
                if c > 0:
                    panel_three(c - 1)
                panel_two(c)
                panel_three(c)
                for j in range(pieces):
                    panel_ready(j)
            last = len(batches) - 1
            if projected == last:
                project(last, 0)
        ahead = (last_piece < c < chunks - 1 and projected < len(batches)
                 and sum(batches[projected]) == (c + 1) * chunk)
        if ahead:
            project(projected, 0)
        stage_image(c)
        if c < pieces and c < chunks - 1:
            if c > 0:
                if c + 1 < chunks:
                    pump(c + 1, 2)
                panel_three(c - 1)
                if c + 2 < chunks:
                    pump(c + 2, 1)
            panel_two(c)
            if c == last_piece:
                if c + 2 < chunks:
                    pump(c + 2, 2)
                early = groups > 1 and batches[0][0] + batches[0][1] == (c + 1) * chunk
                for j in range(pieces - 1):
                    panel_ready(j)
                    if early:
                        project_theirs(0, 0, j)
                        project_theirs(0, 1, j)
                panel_three(c)
                panel_ready(c)
                if early:
                    project_theirs(0, 0, c)
                    project_theirs(0, 1, c)
                    project_ours(0, 0)
                    project_ours(0, 1)
                    projected = 1
        if last_piece <= c < chunks - 1:
            while projected < len(batches) and batches[projected][0] + batches[projected][1] <= (c + 1) * chunk:
                if not ahead:
                    project(projected, 0)
                project(projected, 1)
                projected += 1
    for g in range(projected, len(batches)):
        if g < len(batches) - 1:
            project(g, 0)
        project(g, 1)
    for g in range(len(batches)):
        collect(g, 0)
        collect(g, 1)

    def sent(copy):
        copy.wait_send()

    for c in range(chunks + 1):
        cross(c).wait_send()
        send_plane(c, 0, sent)
        send_plane(c, 1, sent)
        for d in range(1, levels - 1):
            for way in range(2):
                @pl.when(has_source(way, d) & has_target(way))
                def _():
                    sent(relay(c, way, d))
    panel_done()
    for g in range(len(batches)):
        for j in range(groups):
            result_copy(g, 0, j).wait_send()
            result_copy(g, 1, j).wait_send()


def coefficients(nr, nz):
    plane = nr * nz
    window = BLOCK + 2 * nz
    out = np.zeros((plane, 2 * LANES), np.float64)
    for i in range(nr):
        radius = float(nr + i)
        for z in range(nz):
            row = i * nz + z
            first = row // BLOCK * BLOCK - nz
            terms = {}

            def add(ii, zz, value):
                if 0 <= ii < nr:
                    terms[ii * nz + zz] = terms.get(ii * nz + zz, 0.0) + value

            add(i, z, 2.0 + (nr / radius) ** 2 - CENTER)
            add(i, (z + 1) % nz, -0.5)
            add(i, (z - 1) % nz, -0.5)
            add(i + 1, z, -0.5 * (1.0 + 1.0 / (2.0 * radius)))
            add(i - 1, z, -0.5 * (1.0 - 1.0 / (2.0 * radius)))
            for col, value in terms.items():
                out[row, col - first] = value / HALF_SPAN
                out[row, col - first + window] = value / HALF_SPAN
    return out.astype(np.float32)


def shift_matrices(size, nz):
    row = np.arange(size)[:, None]
    col = np.arange(size)[None, :]
    same = row // nz == col // nz
    gap = (col - row) % nz
    return np.stack([same & (gap == nz - TWIST), same & (gap == TWIST)]).astype(np.float32)


def on_device(n, nb, orbitals, potential, near_points, near_values, far_points, far_values, atom_energy):
    _, nr, nz, cols = orbitals.shape
    plane = nr * nz
    atoms = near_points.shape[0]
    mine = cols // 2
    chunk = LANES
    chunks = mine // chunk
    if chunks >= 4:
        batches = [(0, 2 * chunk)] + [(c * chunk, chunk) for c in range(2, chunks)]
    else:
        batches = [(0, mine)]
    rows = PANEL // n
    panel_dev = PANEL // nb
    pieces = max(panel_dev // LANES // 2, 1)
    hops = n // 2 - 1
    tall = plane + 2 * nz
    vmem = pl.BlockSpec(memory_space=pltpu.VMEM)
    dma = pltpu.SemaphoreType.DMA
    given = (orbitals.reshape(plane, cols), near_points, near_values, far_points, far_values,
             atom_energy.reshape(1, atoms), potential.reshape(nr, nz).T,
             jnp.asarray(coefficients(nr, nz)), jnp.asarray(shift_matrices(plane // 2, nz)).astype(BF16))
    return pl.pallas_call(
        functools.partial(kernel, n, nb, nr, nz, chunk, batches),
        out_shape=(jax.ShapeDtypeStruct((rows, cols), F32),) * 2,
        in_specs=[pl.BlockSpec(memory_space=pltpu.HBM)] * len(given),
        out_specs=(vmem,) * 2,
        scratch_shapes=[pltpu.VMEM(array.shape, array.dtype) for array in given] + [
            pltpu.VMEM((n + 2, tall, mine), BF16),
            pltpu.VMEM((n + 2, tall, chunk), BF16),
            pltpu.VMEM((n + 2, tall, mine), BF16),
            pltpu.VMEM((n, plane, mine), BF16),
            pltpu.VMEM((n, 2 * atoms, LANES), F32),
            pltpu.VMEM((n, 2 * atoms, plane), BF16),
            pltpu.VMEM((n, plane, 2 * LANES), BF16),
            pltpu.VMEM((n, atoms, LANES), F32),
            pltpu.VMEM((n, 2 * atoms, chunk), F32),
            pltpu.VMEM((n, 4 * atoms, chunk), BF16),
            pltpu.VMEM((n, plane, panel_dev), BF16),
            pltpu.VMEM((n, panel_dev, plane), BF16),
            pltpu.VMEM((panel_dev, mine), F32),
            pltpu.VMEM((panel_dev, mine), F32),
            pltpu.VMEM((rows, mine), F32),
            pltpu.VMEM((rows, mine), F32),
            dma((chunks + 1,)),
            dma((chunks + 1,)),
            dma((2, chunks + 1, hops, 2)),
            dma((2, chunks + 1, hops, 2)),
            dma((4, pieces, CUTS, nb)),
            dma((4, pieces, CUTS)),
            dma((2, len(batches), pieces)),
            dma((2, len(batches), pieces)),
            dma((len(given),)),
        ],
        compiler_params=pltpu.CompilerParams(
            collective_id=0, has_side_effects=True, vmem_limit_bytes=56 * 2 ** 20
        ),
    )(*given)


def solution(mesh):
    n, nb = mesh.shape["sector"], mesh.shape["band"]
    return jax.shard_map(
        functools.partial(on_device, n, nb),
        mesh=mesh,
        in_specs=(
            P("sector", None, None, "band"),
            P("sector", None, None),
            P("sector", None),
            P("sector", None),
            P("sector", None),
            P("sector", None),
            P("sector"),
        ),
        out_specs=(P("sector", "band"), P("sector", "band")),
        check_vma=False,
    )
```
